128 devices in a mesh: proto: 32 (over z, x, core), rows: 4 (over y).
Axes of the slice: x: 4, y: 4, z: 4, core: 2. Of those that a mesh axis runs over, the one named last changes fastest.
Arguments:
- student_patches: bfloat16 [8192, 256], P('rows'), may hold values from -8 to 8
- teacher_patches: bfloat16 [8192, 256], P('rows'), may hold values from -8 to 8
- mask_index: int32 [4096], P('rows'), may hold values from 0 to 2047
- proto_weight: bfloat16 [131072, 256], P('proto'), may hold values from -1 to 1
- row_cotangent: float32 [4096], P('rows'), may hold values from -6 to 6
Outputs:
- loss: float32 [4096], P('rows')
- grad_patches: float32 [8192, 256], P('rows')
- grad_weight: float32 [131072, 256], P(('proto', 'rows'))
The draws below stay inside these ranges and needn't reach their ends.
Inputs may be any that keep to these rules, and one draw needn't show every extreme that they name: Each entry names one of the 2048 patches of its own row group: row i uses patch (i // 1024) * 2048 + mask_index[i]; entries may repeat.
All inputs are finite; a program needn't handle non-finite values.
Results may differ from the reference program's by a relative error of at most 0.023.
Values may be sent and summed in bfloat16 or wider, within the bound.
A program may use at most 128 MiB of HBM per device.

```python
import math
import jax
import jax.numpy as jnp
from jax import lax

D = 256
PROTO_DEV = 4096
ROWS_DEV = 1024
SWEEPS = 3
PATCH_DEV = 2048
PROTOS = 131072
ROWS = 4096
PATCHES = 8192
N_PROTO = 32
N_ROWS = 4


clusters = 64


def shared_centers(key):
    return jax.random.normal(jax.random.fold_in(key, 100), (clusters, D), jnp.float32) * D ** (-0.5)


def patch_centers(key):
    first_pick = jax.random.randint(jax.random.fold_in(key, 101), (PATCHES,), 0, clusters)
    second_pick = jax.random.randint(jax.random.fold_in(key, 102), (PATCHES,), 0, clusters)
    chosen = jnp.take(shared_centers(key), jnp.minimum(first_pick, second_pick), axis=0)
    return chosen


def proto_clusters(key):
    first_width = jax.random.randint(jax.random.fold_in(key, 104), (clusters,), 1, 5)
    second_width = jax.random.randint(jax.random.fold_in(key, 105), (clusters,), 1, 5)
    widths = (first_width * second_width).astype(jnp.int32)
    ends = (jnp.cumsum(widths) * PROTOS // jnp.sum(widths)).astype(jnp.int32)
    positions = jnp.arange(PROTOS, dtype=jnp.int32)
    passed = (positions[:, None] >= ends[None, :]).astype(jnp.int32)
    return jnp.minimum(jnp.sum(passed, axis=1), clusters - 1).astype(jnp.int32)


def draw_teacher_patches(key, part):
    center_part = patch_centers(key)
    key = jax.random.fold_in(key, 1)
    noise_part = jax.random.normal(jax.random.fold_in(key, 1), (PATCHES, D), jnp.float32) * D ** (-0.5)
    scales = jnp.exp(jax.random.uniform(jax.random.fold_in(key, 2), (PATCHES, 1), jnp.float32, 0.0, math.log(10.0)))
    return jnp.clip((0.8 * center_part + 0.6 * noise_part) * scales, -8.0, 8.0).astype(jnp.bfloat16)


def draw_student_patches(key, part):
    center_part = patch_centers(key)
    key = jax.random.fold_in(key, 2)
    noise_part = jax.random.normal(jax.random.fold_in(key, 1), (PATCHES, D), jnp.float32) * D ** (-0.5)
    scales = jnp.exp(jax.random.uniform(jax.random.fold_in(key, 2), (PATCHES, 1), jnp.float32, 0.0, math.log(10.0)))
    return jnp.clip((0.5 * center_part + 0.6 * noise_part) * scales, -8.0, 8.0).astype(jnp.bfloat16)


def draw_proto_weight(key, part):
    assign = proto_clusters(key)
    center_part = jnp.take(shared_centers(key), assign, axis=0)
    key = jax.random.fold_in(key, 3)
    noise_part = jax.random.normal(jax.random.fold_in(key, 1), (PROTOS, D), jnp.float32) * D ** (-0.5)
    scales = jnp.exp(jax.random.uniform(jax.random.fold_in(key, 2), (PROTOS, 1), jnp.float32, math.log(0.03), math.log(0.3)))
    return jnp.clip((0.8 * center_part + 0.6 * noise_part) * scales, -1.0, 1.0).astype(jnp.bfloat16)


def place_ends(array, own_key, smallest, top_value):
    longest = array.shape.index(max(array.shape))
    spots = []
    for shift in (0, 1):
        where = [jax.random.randint(jax.random.fold_in(own_key, axis), (), 0, length) for axis, length in enumerate(array.shape)]
        where[longest] = (where[longest] + shift) % array.shape[longest]
        spots.append(tuple(where))
    return array.at[spots[0]].set(smallest).at[spots[1]].set(top_value)


def shard_levels(key, extent, pieces, low, largest):
    level, own = 1.0, jax.random.fold_in(key, 6)
    for position, blocks in pieces:
        heights = jnp.exp(jax.random.uniform(jax.random.fold_in(own, position), (blocks,), jnp.float32, low / len(pieces), largest / len(pieces)))
        level = level * jnp.repeat(heights, extent[position] // blocks).reshape([-1 if axis == position else 1 for axis in range(len(extent))])
    return level


def centred(key, dims, deviation, reach, pieces=(), kind=jnp.bfloat16):
    entries = deviation * jax.random.normal(key, dims, jnp.float32)
    if pieces:
        entries = entries * shard_levels(key, dims, pieces, -0.22, 0.18)
    return jnp.clip(entries, -reach, reach).astype(kind)


def setup_inputs(seed: int = 0) -> dict:
    key_of = jax.random.split(jax.random.key(seed), 6)
    return {
        "student_patches": draw_student_patches(jax.random.fold_in(key_of[5], 71), 0),
        "teacher_patches": draw_teacher_patches(jax.random.fold_in(key_of[5], 71), 0),
        "mask_index": place_ends(jax.random.randint(key_of[2], (ROWS,), 0, PATCH_DEV), jax.random.fold_in(key_of[2], 1), 0, PATCH_DEV - 1).astype(jnp.int32),
        "proto_weight": draw_proto_weight(jax.random.fold_in(key_of[5], 71), 0),
        "row_cotangent": centred(key_of[4], (ROWS,), 1.0, 6.0, ((0, 4),), jnp.float32),
    }


teacher_temp = 0.07
student_temp = 0.1
epsilon = 1e-06

def unit_rows(values):
    scale_rows = lax.rsqrt(lax.optimization_barrier(jnp.sum(values * values, axis=1, keepdims=True)) + epsilon)
    return (values * scale_rows, scale_rows)

def reference(student_patches, teacher_patches, mask_index, proto_weight, row_cotangent):
    row_group = jnp.arange(ROWS, dtype=jnp.int32) // ROWS_DEV
    patch_index = (row_group * PATCH_DEV + mask_index).astype(jnp.int32)
    student_rows = jnp.take(student_patches, patch_index, axis=0).astype(jnp.float32)
    teacher_rows = jnp.take(teacher_patches, patch_index, axis=0).astype(jnp.float32)
    student_unit, student_scale = unit_rows(student_rows)
    student_half = student_unit.astype(jnp.bfloat16)
    teacher_unit, teacher_scale = unit_rows(teacher_rows)
    teacher_half = teacher_unit.astype(jnp.bfloat16)
    weight_unit, weight_scale = unit_rows(proto_weight.astype(jnp.float32))
    weight_half = weight_unit.astype(jnp.bfloat16)
    half_blocks = weight_half.reshape(N_PROTO, PROTO_DEV, D)
    unit_blocks = weight_unit.reshape(N_PROTO, PROTO_DEV, D)
    scale_blocks = weight_scale.reshape(N_PROTO, PROTO_DEV, 1)

    def teacher_block(weight_block):
        return jnp.exp(jnp.dot(teacher_half, weight_block.T, preferred_element_type=jnp.float32) / teacher_temp)
    transport = lax.map(teacher_block, half_blocks)
    for repeat in range(SWEEPS):
        transport = transport / (lax.optimization_barrier(jnp.sum(transport, axis=1, keepdims=True)) * PROTOS)
        transport = transport / (lax.optimization_barrier(jnp.sum(transport, axis=(0, 2), keepdims=True)) * ROWS)
    targets = transport * ROWS

    def student_block(weight_block):
        return jnp.dot(student_half, weight_block.T, preferred_element_type=jnp.float32) / student_temp

    def forward_step(totals, inputs_step):
        weight_block, target_block = inputs_step
        logits = student_block(weight_block)
        return ((totals[0] + lax.optimization_barrier(jnp.sum(jnp.exp(logits), axis=1)), totals[1] + lax.optimization_barrier(jnp.sum(target_block * logits, axis=1))), None)
    zero_rows = jnp.zeros((ROWS,), jnp.float32)
    (expo_total, cross), ignored = lax.scan(forward_step, (zero_rows, zero_rows), (half_blocks, targets))
    loss = jnp.log(expo_total) - cross

    def backward_step(grad_unit, inputs_step):
        weight_block, unit_block, scale_block, target_block = inputs_step
        logits = student_block(weight_block)
        student_probs = jnp.exp(logits) / expo_total[:, None]
        grad_scores = (row_cotangent[:, None] * (student_probs - target_block) / student_temp).astype(jnp.bfloat16)
        grad_unit = grad_unit + jnp.dot(grad_scores, weight_block, preferred_element_type=jnp.float32)
        group_parts = jnp.einsum('grk,grd->gkd', grad_scores.reshape(N_ROWS, ROWS_DEV, PROTO_DEV).astype(jnp.float32), student_half.reshape(N_ROWS, ROWS_DEV, D).astype(jnp.float32))
        rounded = lax.optimization_barrier(group_parts.astype(jnp.bfloat16))
        grad_weight_unit = lax.optimization_barrier(jnp.sum(rounded.astype(jnp.float32), axis=0))
        grad_block = (grad_weight_unit - unit_block * lax.optimization_barrier(jnp.sum(unit_block * grad_weight_unit, axis=1, keepdims=True))) * scale_block
        return (grad_unit, grad_block)
    grad_unit, grad_blocks = lax.scan(backward_step, jnp.zeros((ROWS, D), jnp.float32), (half_blocks, unit_blocks, scale_blocks, targets))
    grad_rows = (grad_unit - student_unit * lax.optimization_barrier(jnp.sum(student_unit * grad_unit, axis=1, keepdims=True))) * student_scale
    grad_patches = jnp.zeros((PATCHES, D), jnp.float32).at[patch_index].add(grad_rows)
    return (loss, grad_patches, grad_blocks.reshape(PROTOS, D))
```

```python
import jax
import jax.numpy as jnp
from jax import lax
from jax.experimental import pallas as pl
from jax.experimental.pallas import tpu as pltpu
from jax.sharding import PartitionSpec as P

teacher_temp = 0.07
student_temp = 0.1
epsilon = 1e-06

f32, bf16 = jnp.float32, jnp.bfloat16
MESH = pl.DeviceIdType.MESH
NN = (((1,), (0,)), ((), ()))
NT = (((1,), (1,)), ((), ()))
TN = (((0,), (0,)), ((), ()))

D = 256
LANES = 128
BLOCK = 256
WIDE = 512


def dot(left, right, dims):
    return lax.dot_general(left, right, dims, preferred_element_type=f32)


def fold(row):
    count = row.shape[1] // LANES
    return jnp.concatenate([row[:, i * LANES : (i + 1) * LANES] for i in range(count)], axis=0)


def unfold(square):
    return jnp.concatenate([square[i : i + 1, :] for i in range(square.shape[0])], axis=1)


def high_low(row):
    high = row.astype(bf16).astype(f32)
    return jnp.concatenate(
        [high, row - high, jnp.zeros((6, row.shape[1]), f32)], axis=0
    ).astype(bf16)


def column_of(square):
    count = square.shape[0]
    padded = jnp.concatenate([square, jnp.zeros((LANES - count, LANES), f32)], axis=0)
    turned = padded.T
    return jnp.concatenate([turned[:, i : i + 1] for i in range(count)], axis=0)


def make_kernel(n_proto, n_rows, rows, patches, protos):
    all_rows = float(rows * n_rows)
    all_protos = float(protos * n_proto)
    keep = protos // n_rows
    row_tiles = rows // LANES
    proto_tiles = protos // LANES
    keep_tiles = keep // LANES
    half = rows // 2
    pairs = n_proto // 2
    chunk = D // pairs
    others = n_rows - 1

    def kernel(
        sp_any, tp_any, idx_ref, w_any, rc_ref,
        loss_ref, gp_ref, gw_ref,
        sp_ref, tp_ref, w_ref,
        onehot, wh, wht, plan, expo, tt, srt, sht, scaled, part, csum, vbuf,
        cbuf, rbuf, r3buf, fbuf,
        ot, os, planx, cpart,
        asend, arecv, axs, axr, bsend, brecv, bxs, bxr, dfull,
        in_s, y_s, y_r, p_s, p_r, f_s, f_r,
        gy_s, gy_r, gz_s, gz_r, gc_s, gc_r,
        s_s, s_r, x_s, x_r,
    ):
        p = lax.axis_index("proto")
        y = lax.axis_index("rows")
        pair = lax.div(p, 2)
        core = lax.rem(p, 2)

        barrier = pltpu.get_barrier_semaphore()

        def greet(d, carry):
            pl.semaphore_signal(
                barrier, inc=1, device_id=(lax.rem(p + d, n_proto), y), device_id_type=MESH
            )
            return carry

        for d in range(1, n_rows):
            pl.semaphore_signal(
                barrier, inc=1, device_id=(p, lax.rem(y + d, n_rows)), device_id_type=MESH
            )
        lax.fori_loop(1, n_proto, greet, 0)

        fetch_t = pltpu.make_async_copy(tp_any, tp_ref, in_s.at[0])
        fetch_w = pltpu.make_async_copy(w_any, w_ref, in_s.at[1])
        fetch_s = pltpu.make_async_copy(sp_any, sp_ref, in_s.at[2])
        fetch_t.start()
        fetch_w.start()
        fetch_s.start()

        def remote(source, target, send, recv, device):
            return pltpu.make_async_remote_copy(
                src_ref=source, dst_ref=target, send_sem=send, recv_sem=recv,
                device_id=device, device_id_type=MESH,
            )

        def to_plane(d):
            return (lax.rem(p + d, n_proto), y)

        def to_core(d):
            return (lax.rem(p + 2 * d, n_proto), y)

        def to_row(d):
            return (p, lax.rem(y + d, n_rows))

        sibling = (p + 1 - 2 * core, y)

        def each(count, copy_of, act):
            def body(d, carry):
                act(copy_of(d))
                return carry

            lax.fori_loop(1, count, body, 0)

        def start(copy):
            copy.start()

        def wait(copy):
            copy.wait()

        def totals(buf, e):
            return lambda d: remote(buf.at[p], buf.at[p], p_s.at[e, d], p_r.at[e, d], to_plane(d))

        def columns(e):
            return lambda d: remote(
                cbuf.at[e, y], cbuf.at[e, y], y_s.at[e, d], y_r.at[e, d], to_row(d)
            )

        def factors(e):
            return lambda d: remote(
                fbuf.at[e, y], fbuf.at[e, y], f_s.at[e, d], f_r.at[e, d], to_row(d)
            )

        def row_each(copy_of, act):
            for d in range(1, n_rows):
                act(copy_of(d))

        def sum_slots(buf, count):
            total = buf[0].astype(f32)
            for i in range(1, count):
                total = total + buf[i].astype(f32)
            return total

        features = pl.ds(pl.multiple_of(pair * chunk, chunk), chunk)
        my_half = pl.ds(pl.multiple_of(core * half, half), half)
        other_half = pl.ds(pl.multiple_of((1 - core) * half, half), half)

        def group_row(e, own, far):
            return lambda d: remote(
                own.at[features, my_half], far.at[d - 1, features, my_half],
                gy_s.at[e, d], gy_r.at[e, d], to_row(d),
            )

        def group_core(e, far):
            piece = far.at[:, features, my_half]
            return lambda d: remote(piece, piece, gz_s.at[e, d], gz_r.at[e, d], to_core(d))

        def group_pair(e, far):
            piece = far.at[:, :, my_half]
            return remote(piece, piece, gc_s.at[e], gc_r.at[e], sibling)

        idx_row = unfold(idx_ref[...])
        for i in range(patches // BLOCK):
            spot = lax.broadcasted_iota(jnp.int32, (BLOCK, rows), 0) + i * BLOCK
            onehot[i * BLOCK : (i + 1) * BLOCK, :] = (spot == idx_row).astype(bf16)
        fetch_t.wait()
        teacher = dot(tp_ref[...], onehot[...], TN)
        tt[...] = (
            teacher * lax.rsqrt(jnp.sum(teacher * teacher, axis=0, keepdims=True) + epsilon)
        ).astype(bf16)

        ones = jnp.ones((8, LANES), bf16)
        fetch_w.wait()

        def plan_block(i, carry):
            at = pl.ds(pl.multiple_of(i * WIDE, WIDE), WIDE)
            block = w_ref[at, :].astype(f32)
            scale = lax.rsqrt(jnp.sum(block * block, axis=1, keepdims=True) + epsilon)
            unit = (block * scale).astype(bf16)
            wh[at, :] = unit
            wht[:, at] = unit.T
            values = jnp.exp(dot(unit, tt[...], NN) * (1.0 / teacher_temp))
            plan[at, :] = values.astype(bf16)
            lane_sum = values[:, :LANES]
            for j in range(1, row_tiles):
                lane_sum = lane_sum + values[:, j * LANES : (j + 1) * LANES]
            high = lane_sum.astype(bf16)
            low = (lane_sum - high.astype(f32)).astype(bf16)
            csum[:, at] = dot(ones, high, NT) + dot(ones, low, NT)
            return carry

        lax.fori_loop(0, protos // WIDE, plan_block, 0, unroll=2)
        pl.semaphore_wait(barrier, n_proto - 1 + n_rows - 1)

        def columns_begin(e, sums):
            cbuf[e, y] = fold(sums)
            row_each(columns(e), start)

        def columns_end(e):
            row_each(columns(e), wait)
            total = cbuf[e, 0]
            for i in range(1, n_rows):
                total = total + cbuf[e, i]
            return 1.0 / (all_protos * total)

        def row_sums(v):
            sums = dot(high_low(unfold(v)), plan[...], NN)
            return fold(sums[0:1, :] + sums[1:2, :])

        def column_sums(u):
            sums = dot(high_low(unfold(u)), plan[...], NT)
            return sums[0:1, :] + sums[1:2, :]

        def student_block(i, carry):
            at = pl.ds(pl.multiple_of(i * WIDE, WIDE), WIDE)
            values = jnp.exp(dot(wh[at, :], sht[...], NN) * (1.0 / student_temp))
            expo[at, :] = values.astype(bf16)
            return carry + jnp.sum(values.reshape(WIDE // 8, 8, rows), axis=0)

        columns_begin(0, csum[0:1, :])
        row_each(group_row(0, tt, ot), start)
        fetch_s.wait()
        student = dot(sp_ref[...], onehot[...], TN)
        scale_s = lax.rsqrt(jnp.sum(student * student, axis=0, keepdims=True) + epsilon)
        srt[...] = student.astype(bf16)
        sht[...] = (student * scale_s).astype(bf16)
        row_each(group_row(1, sht, os), start)
        v = columns_end(0)
        rbuf[0, p] = row_sums(v)
        each(n_proto, totals(rbuf.at[0], 0), start)
        row_each(group_row(0, tt, ot), wait)
        each(pairs, group_core(0, ot), start)
        expo_rows = lax.fori_loop(
            0, protos // WIDE, student_block, jnp.zeros((8, rows), f32), unroll=2
        )
        rbuf[2, p] = fold(jnp.sum(expo_rows, axis=0, keepdims=True))
        each(n_proto, totals(rbuf.at[0], 0), wait)
        u = 1.0 / (all_rows * sum_slots(rbuf.at[0], n_proto))

        columns_begin(1, column_sums(u))
        part[...] = dot(wht[...], expo[...], NN)

        def fold_pair(xs, xr, e):
            xs[...] = part[:, other_half].astype(bf16)
            return remote(xs, xr, x_s.at[e], x_r.at[e], sibling)

        def fold_core(send, recv, e):
            return lambda d: remote(
                send.at[lax.rem(pair + d, pairs)], recv.at[pair],
                s_s.at[e, d], s_r.at[e, d], to_core(d),
            )

        def fold_begin(xr, send, recv, e):
            total = part[:, my_half] + xr[...].astype(f32)
            send[...] = total.reshape(pairs, chunk, half).astype(bf16)
            recv[pair] = send[pair]
            each(pairs, fold_core(send, recv, e), start)

        a_pair = fold_pair(axs, axr, 0)
        a_pair.start()
        v = columns_end(1)
        rbuf[1, p] = row_sums(v)
        each(n_proto, totals(rbuf.at[1], 1), start)
        each(n_proto, totals(rbuf.at[2], 2), start)
        each(pairs, group_core(0, ot), wait)
        t_pair = group_pair(0, ot)
        t_pair.start()
        row_each(group_row(1, sht, os), wait)
        each(pairs, group_core(1, os), start)
        a_pair.wait()
        fold_begin(axr, asend, arecv, 0)
        t_pair.wait()
        def quarter(d):
            return pl.ds(pl.multiple_of(lax.rem(y + d, n_rows) * keep, keep), keep)

        mine = quarter(0)
        for d in range(others):
            values = jnp.exp(dot(wh[mine, :], ot[d], NN) * (1.0 / teacher_temp))
            planx[d] = values.astype(bf16)
        each(n_proto, totals(rbuf.at[1], 1), wait)
        u = 1.0 / (all_rows * sum_slots(rbuf.at[1], n_proto))

        columns_begin(2, column_sums(u))
        each(n_proto, totals(rbuf.at[2], 2), wait)
        expo_total = sum_slots(rbuf.at[2], n_proto)
        cot = rc_ref[...] * (1.0 / student_temp)
        over_expo = cot / expo_total
        fbuf[0, y] = over_expo
        row_each(factors(0), start)
        each(pairs, group_core(1, os), wait)
        s_pair = group_pair(1, os)
        s_pair.start()
        each(pairs, fold_core(asend, arecv, 0), wait)
        v = columns_end(2)
        vbuf[...] = v
        part[...] = dot((wht[...].astype(f32) * unfold(v)).astype(bf16), plan[...], NN)
        b_pair = fold_pair(bxs, bxr, 1)
        b_pair.start()
        r3buf[p] = jnp.concatenate(
            [
                row_sums(v),
                fold(jnp.sum(part[...] * sht[...].astype(f32), axis=0, keepdims=True)),
            ],
            axis=0,
        )
        each(n_proto, totals(r3buf, 3), start)
        b_pair.wait()
        fold_begin(bxr, bsend, brecv, 1)

        s_pair.wait()
        row_each(factors(0), wait)
        for d in range(others):
            values = jnp.exp(dot(wh[mine, :], os[d], NN) * (1.0 / student_temp))
            expo[quarter(d + 1), :] = values.astype(bf16)

        def contract(own, far, e):
            scaled[0] = (sht[...].astype(f32) * unfold(fbuf[e, y])).astype(bf16)
            total = dot(own[mine, :], scaled[0], NT)
            for d in range(1, n_rows):
                factor = unfold(fbuf[e, lax.rem(y + n_rows - d, n_rows)])
                scaled[d] = (os[d - 1].astype(f32) * factor).astype(bf16)
                total = total + dot(far(d), scaled[d], NT)
            return total

        cpart[...] = contract(expo, lambda d: expo[quarter(d), :], 0)
        each(n_proto, totals(r3buf, 3), wait)
        both = sum_slots(r3buf, n_proto)
        inverse = 1.0 / both[:row_tiles]
        loss_ref[:row_tiles] = jnp.log(expo_total)
        loss_ref[row_tiles:] = both[row_tiles:] * inverse * (1.0 / student_temp)
        over_rows = cot * inverse
        fbuf[1, y] = over_rows
        row_each(factors(1), start)

        a_total = sum_slots(arecv, pairs)
        each(pairs, fold_core(bsend, brecv, 1), wait)
        b_total = sum_slots(brecv, pairs)

        def half_row(square):
            row = unfold(square)
            return jnp.where(core == 0, row[:, :half], row[:, half:])

        dfull[features, my_half] = (
            a_total * half_row(over_expo) - b_total * half_row(over_rows)
        ).astype(bf16)
        own_piece = dfull.at[features, my_half]
        spread = lambda d: remote(own_piece, own_piece, s_s.at[2, d], s_r.at[2, d], to_core(d))
        each(pairs, spread, start)

        row_each(factors(1), wait)
        column = column_of(vbuf[pl.ds(pl.multiple_of(y * keep_tiles, keep_tiles), keep_tiles), :])
        total = cpart[...] - column * contract(plan, lambda d: planx[d - 1], 1)
        kept = w_ref[mine, :].astype(f32)
        scale_w = lax.rsqrt(jnp.sum(kept * kept, axis=1, keepdims=True) + epsilon)
        unit_w = kept * scale_w
        gw_ref[...] = (
            (total - unit_w * jnp.sum(unit_w * total, axis=1, keepdims=True)) * scale_w
        ).astype(bf16)

        each(pairs, spread, wait)
        my_pieces = dfull.at[:, my_half]
        d_pair = remote(my_pieces, my_pieces, x_s.at[2], x_r.at[2], sibling)
        d_pair.start()
        d_pair.wait()
        grad_unit = dfull[...].astype(f32)
        unit = srt[...].astype(f32) * scale_s
        grad_rows = (
            grad_unit - unit * jnp.sum(unit * grad_unit, axis=0, keepdims=True)
        ) * scale_s
        gp_ref[...] = dot(onehot[...], grad_rows.astype(bf16), NT).astype(bf16)

    scratch = [
        pltpu.VMEM((patches, D), bf16),
        pltpu.VMEM((patches, D), bf16),
        pltpu.VMEM((protos, D), bf16),
        pltpu.VMEM((patches, rows), bf16),
        pltpu.VMEM((protos, D), bf16),
        pltpu.VMEM((D, protos), bf16),
        pltpu.VMEM((protos, rows), bf16),
        pltpu.VMEM((protos, rows), bf16),
        pltpu.VMEM((D, rows), bf16),
        pltpu.VMEM((D, rows), bf16),
        pltpu.VMEM((D, rows), bf16),
        pltpu.VMEM((n_rows, D, rows), bf16),
        pltpu.VMEM((D, rows), f32),
        pltpu.VMEM((8, protos), f32),
        pltpu.VMEM((proto_tiles, LANES), f32),
        pltpu.VMEM((3, n_rows, proto_tiles, LANES), f32),
        pltpu.VMEM((3, n_proto, row_tiles, LANES), f32),
        pltpu.VMEM((n_proto, 2 * row_tiles, LANES), f32),
        pltpu.VMEM((2, n_rows, row_tiles, LANES), f32),
        pltpu.VMEM((others, D, rows), bf16),
        pltpu.VMEM((others, D, rows), bf16),
        pltpu.VMEM((others, keep, rows), bf16),
        pltpu.VMEM((keep, D), f32),
        pltpu.VMEM((pairs, chunk, half), bf16),
        pltpu.VMEM((pairs, chunk, half), bf16),
        pltpu.VMEM((D, half), bf16),
        pltpu.VMEM((D, half), bf16),
        pltpu.VMEM((pairs, chunk, half), bf16),
        pltpu.VMEM((pairs, chunk, half), bf16),
        pltpu.VMEM((D, half), bf16),
        pltpu.VMEM((D, half), bf16),
        pltpu.VMEM((D, rows), bf16),
        pltpu.SemaphoreType.DMA((3,)),
        pltpu.SemaphoreType.DMA((3, n_rows)),
        pltpu.SemaphoreType.DMA((3, n_rows)),
        pltpu.SemaphoreType.DMA((4, n_proto)),
        pltpu.SemaphoreType.DMA((4, n_proto)),
        pltpu.SemaphoreType.DMA((2, n_rows)),
        pltpu.SemaphoreType.DMA((2, n_rows)),
        pltpu.SemaphoreType.DMA((2, n_rows)),
        pltpu.SemaphoreType.DMA((2, n_rows)),
        pltpu.SemaphoreType.DMA((2, pairs)),
        pltpu.SemaphoreType.DMA((2, pairs)),
        pltpu.SemaphoreType.DMA((2,)),
        pltpu.SemaphoreType.DMA((2,)),
        pltpu.SemaphoreType.DMA((3, pairs)),
        pltpu.SemaphoreType.DMA((3, pairs)),
        pltpu.SemaphoreType.DMA((3,)),
        pltpu.SemaphoreType.DMA((3,)),
    ]
    return kernel, scratch


def shards(student_patches, teacher_patches, mask_index, proto_weight, row_cotangent):
    n_proto, n_rows = lax.axis_size("proto"), lax.axis_size("rows")
    rows = mask_index.shape[0]
    patches = student_patches.shape[0]
    protos = proto_weight.shape[0]
    kernel, scratch = make_kernel(n_proto, n_rows, rows, patches, protos)
    vmem = pl.BlockSpec(memory_space=pltpu.VMEM)
    anywhere = pl.BlockSpec(memory_space=pl.ANY)
    terms, grad_patches, grad_weight = pl.pallas_call(
        kernel,
        out_shape=(
            jax.ShapeDtypeStruct((2 * rows // LANES, LANES), f32),
            jax.ShapeDtypeStruct((patches, D), bf16),
            jax.ShapeDtypeStruct((protos // n_rows, D), bf16),
        ),
        in_specs=[anywhere, anywhere, vmem, anywhere, vmem],
        out_specs=(vmem, vmem, vmem),
        scratch_shapes=scratch,
        compiler_params=pltpu.CompilerParams(
            collective_id=0, has_side_effects=True, vmem_limit_bytes=60 << 20
        ),
    )(
        student_patches,
        teacher_patches,
        mask_index.reshape(rows // LANES, LANES),
        proto_weight,
        row_cotangent.reshape(rows // LANES, LANES),
    )
    tiles = rows // LANES
    loss = (terms[:tiles] - terms[tiles:]).reshape(rows)
    return loss, grad_patches.astype(f32), grad_weight.astype(f32)


def solution(mesh):
    in_specs = (P("rows", None), P("rows", None), P("rows"), P("proto", None), P("rows"))
    out_specs = (P("rows"), P("rows", None), P(("proto", "rows"), None))
    return jax.shard_map(shards, mesh=mesh, in_specs=in_specs, out_specs=out_specs, check_vma=False)
```

```python
import itertools
import math

import jax
import jax.numpy as jnp
from jax import lax
from jax.experimental import pallas as pl
from jax.experimental.pallas import tpu as pltpu
from jax.sharding import PartitionSpec as P

teacher_temp = 0.07
student_temp = 0.1
epsilon = 1e-06

f32, bf16 = jnp.float32, jnp.bfloat16
MESH = pl.DeviceIdType.MESH
NN = (((1,), (0,)), ((), ()))
NT = (((1,), (1,)), ((), ()))
TN = (((0,), (0,)), ((), ()))

D = 256
LANES = 128
BLOCK = 256
WIDE = 512


def dot(left, right, dims):
    return lax.dot_general(left, right, dims, preferred_element_type=f32)


def fold(row):
    count = row.shape[1] // LANES
    return jnp.concatenate([row[:, i * LANES : (i + 1) * LANES] for i in range(count)], axis=0)


def unfold(square):
    return jnp.concatenate([square[i : i + 1, :] for i in range(square.shape[0])], axis=1)


def high_low(row):
    high = row.astype(bf16).astype(f32)
    return jnp.concatenate(
        [high, row - high, jnp.zeros((6, row.shape[1]), f32)], axis=0
    ).astype(bf16)


def column_of(square):
    count = square.shape[0]
    padded = jnp.concatenate([square, jnp.zeros((LANES - count, LANES), f32)], axis=0)
    turned = padded.T
    return jnp.concatenate([turned[:, i : i + 1] for i in range(count)], axis=0)


def make_kernel(n_proto, n_rows, rows, patches, protos):
    all_rows = float(rows * n_rows)
    all_protos = float(protos * n_proto)
    keep = protos // n_rows
    row_tiles = rows // LANES
    proto_tiles = protos // LANES
    keep_tiles = keep // LANES
    half = rows // 2
    pairs = n_proto // 2
    chunk = D // pairs
    others = n_rows - 1
    side = math.isqrt(pairs)
    assert side * side == pairs and rows == keep

    def hops(offset):
        return sum(min(step, side - step) for step in offset[:2])

    every = itertools.product(range(side), range(side), range(2))
    plane_offsets = sorted((o for o in every if any(o)), key=hops, reverse=True)
    core_offsets = [o for o in plane_offsets if o[2] == 0]
    row_offsets = sorted(range(1, n_rows), key=lambda d: -min(d, n_rows - d))

    def kernel(
        sp_any, tp_any, idx_ref, w_any, rc_ref,
        loss_ref, gr_ref, gw_ref,
        sp_ref, tp_ref, w_ref,
        shared, wh, wht, plan, expo, tt, srt, sht, scaled, part, csum, vbuf,
        cbuf, rbuf, r3buf, fbuf,
        ot, os, cpart,
        asend, arecv, axs, axr, bsend, brecv, bxs, bxr, dfull,
        in_s, y_s, y_r, p_s, p_r, f_s, f_r,
        gy_s, gy_r, gz_s, gz_r, gc_s, gc_r,
        s_s, s_r, x_s, x_r,
    ):
        p = lax.axis_index("proto")
        y = lax.axis_index("rows")
        pair = lax.div(p, 2)
        core = lax.rem(p, 2)
        z = lax.div(pair, side)
        x = lax.rem(pair, side)

        def pair_at(offset):
            return lax.rem(z + offset[0], side) * side + lax.rem(x + offset[1], side)

        def in_plane(offset):
            return (pair_at(offset) * 2 + lax.rem(core + offset[2], 2), y)

        def to_row(d):
            return (p, lax.rem(y + d, n_rows))

        sibling = (p + 1 - 2 * core, y)

        barrier = pltpu.get_barrier_semaphore()
        for offset in plane_offsets:
            pl.semaphore_signal(
                barrier, inc=1, device_id=in_plane(offset), device_id_type=MESH
            )
        for d in range(1, n_rows):
            pl.semaphore_signal(barrier, inc=1, device_id=to_row(d), device_id_type=MESH)

        fetch_t = pltpu.make_async_copy(tp_any, tp_ref, in_s.at[0])
        fetch_w = pltpu.make_async_copy(w_any, w_ref, in_s.at[1])
        fetch_s = pltpu.make_async_copy(sp_any, sp_ref, in_s.at[2])
        fetch_t.start()
        fetch_w.start()
        fetch_s.start()

        def remote(source, target, send, recv, device):
            return pltpu.make_async_remote_copy(
                src_ref=source, dst_ref=target, send_sem=send, recv_sem=recv,
                device_id=device, device_id_type=MESH,
            )

        def arrived(landing, send, recv):
            pltpu.make_async_copy(landing, landing, recv).wait()
            pltpu.make_async_copy(landing, landing, send).wait()

        def totals_begin(buf, e):
            for offset in plane_offsets:
                remote(buf.at[p], buf.at[p], p_s.at[e], p_r.at[e], in_plane(offset)).start()

        def totals_end(buf, e):
            arrived(buf.at[pl.ds(0, n_proto - 1)], p_s.at[e], p_r.at[e])

        def rows_begin(buf, send, recv):
            for d in row_offsets:
                remote(buf.at[y], buf.at[y], send, recv, to_row(d)).start()

        def rows_end(buf, send, recv):
            arrived(buf.at[pl.ds(0, others)], send, recv)

        def sum_slots(buf, count):
            total = buf[0].astype(f32)
            for i in range(1, count):
                total = total + buf[i].astype(f32)
            return total

        features = pl.ds(pl.multiple_of(pair * chunk, chunk), chunk)
        my_half = pl.ds(pl.multiple_of(core * half, half), half)
        other_half = pl.ds(pl.multiple_of((1 - core) * half, half), half)
        all_but_one = pl.ds(0, (pairs - 1) * chunk)

        def group_row_begin(e, own, far):
            for d in row_offsets:
                remote(
                    own.at[features, my_half], far.at[d - 1, features, my_half],
                    gy_s.at[e], gy_r.at[e], to_row(d),
                ).start()

        def group_row_end(e, far):
            arrived(far.at[:, features, my_half], gy_s.at[e], gy_r.at[e])

        def group_core_begin(e, far):
            piece = far.at[:, features, my_half]
            for offset in core_offsets:
                remote(piece, piece, gz_s.at[e], gz_r.at[e], in_plane(offset)).start()

        def group_core_end(e, far):
            arrived(far.at[:, all_but_one, my_half], gz_s.at[e], gz_r.at[e])

        def group_pair(e, far):
            piece = far.at[:, :, my_half]
            return remote(piece, piece, gc_s.at[e], gc_r.at[e], sibling)

        idx_row = unfold(idx_ref[...])
        for i in range(patches // rows):
            spot = lax.broadcasted_iota(jnp.int32, (rows, rows), 0) + i * rows
            shared[i] = (spot == idx_row).astype(bf16)

        def masked(patch_ref):
            total = dot(patch_ref[:rows, :], shared[0], TN)
            for i in range(1, patches // rows):
                total = total + dot(patch_ref[i * rows : (i + 1) * rows, :], shared[i], TN)
            return total

        fetch_t.wait()
        teacher = masked(tp_ref)
        tt[...] = (
            teacher * lax.rsqrt(jnp.sum(teacher * teacher, axis=0, keepdims=True) + epsilon)
        ).astype(bf16)

        ones = jnp.ones((8, LANES), bf16)
        fetch_w.wait()

        def plan_block(i, carry):
            at = pl.ds(pl.multiple_of(i * WIDE, WIDE), WIDE)
            block = w_ref[at, :].astype(f32)
            scale = lax.rsqrt(jnp.sum(block * block, axis=1, keepdims=True) + epsilon)
            unit = (block * scale).astype(bf16)
            wh[at, :] = unit
            wht[:, at] = unit.T
            values = jnp.exp(dot(unit, tt[...], NN) * (1.0 / teacher_temp))
            plan[at, :] = values.astype(bf16)
            lane_sum = values[:, :LANES]
            for j in range(1, row_tiles):
                lane_sum = lane_sum + values[:, j * LANES : (j + 1) * LANES]
            high = lane_sum.astype(bf16)
            low = (lane_sum - high.astype(f32)).astype(bf16)
            csum[:, at] = dot(ones, high, NT) + dot(ones, low, NT)
            return carry

        lax.fori_loop(0, protos // WIDE, plan_block, 0, unroll=2)
        pl.semaphore_wait(barrier, n_proto - 1 + n_rows - 1)

        def columns_begin(e, sums):
            cbuf[e, y] = fold(sums)
            rows_begin(cbuf.at[e], y_s.at[e], y_r.at[e])

        def columns_end(e):
            rows_end(cbuf.at[e], y_s.at[e], y_r.at[e])
            total = cbuf[e, 0]
            for i in range(1, n_rows):
                total = total + cbuf[e, i]
            return 1.0 / (all_protos * total)

        def row_sums(v):
            sums = dot(high_low(unfold(v)), plan[...], NN)
            return fold(sums[0:1, :] + sums[1:2, :])

        def column_sums(u):
            parts = high_low(unfold(u))
            sums = jnp.concatenate(
                [dot(parts, shared[i], NN) for i in range(n_rows)], axis=1
            )
            return sums[0:1, :] + sums[1:2, :]

        def turn(i, carry):
            at = pl.ds(pl.multiple_of(i * BLOCK, BLOCK), BLOCK)
            to = pl.ds(pl.multiple_of(lax.rem(i, keep // BLOCK) * BLOCK, BLOCK), BLOCK)
            shared[lax.div(i, keep // BLOCK), :, to] = plan[at, :].T
            return carry

        turns = protos // BLOCK

        def student_block(i, carry):
            at = pl.ds(pl.multiple_of(i * WIDE, WIDE), WIDE)
            values = jnp.exp(dot(wh[at, :], sht[...], NN) * (1.0 / student_temp))
            expo[at, :] = values.astype(bf16)
            return carry + jnp.sum(values.reshape(WIDE // 8, 8, rows), axis=0)

        columns_begin(0, csum[0:1, :])
        group_row_begin(0, tt, ot)
        fetch_s.wait()
        student = masked(sp_ref)
        scale_s = lax.rsqrt(jnp.sum(student * student, axis=0, keepdims=True) + epsilon)
        srt[...] = student.astype(bf16)
        sht[...] = (student * scale_s).astype(bf16)
        lax.fori_loop(0, turns // 2, turn, 0, unroll=2)
        v = columns_end(0)
        rbuf[0, p] = row_sums(v)
        totals_begin(rbuf.at[0], 0)
        group_row_begin(1, sht, os)
        expo_rows = lax.fori_loop(
            0, protos // WIDE, student_block, jnp.zeros((8, rows), f32), unroll=2
        )
        lax.fori_loop(turns // 2, turns, turn, 0, unroll=2)
        rbuf[2, p] = fold(jnp.sum(expo_rows, axis=0, keepdims=True))
        totals_end(rbuf.at[0], 0)
        u = 1.0 / (all_rows * sum_slots(rbuf.at[0], n_proto))

        columns_begin(1, column_sums(u))
        group_row_end(0, ot)
        group_core_begin(0, ot)
        part[...] = dot(wht[...], expo[...], NN)

        def fold_pair(xs, xr, e):
            xs[...] = part[:, other_half].astype(bf16)
            return remote(xs, xr, x_s.at[e], x_r.at[e], sibling)

        def fold_begin(xr, send, recv, e):
            total = part[:, my_half] + xr[...].astype(f32)
            send[...] = total.reshape(pairs, chunk, half).astype(bf16)
            for offset in core_offsets:
                remote(
                    send.at[pair_at(offset)], recv.at[pair], s_s.at[e], s_r.at[e],
                    in_plane(offset),
                ).start()
            recv[pair] = send[pair]

        def fold_end(recv, e):
            arrived(recv.at[pl.ds(0, pairs - 1)], s_s.at[e], s_r.at[e])
            return sum_slots(recv, pairs)

        a_pair = fold_pair(axs, axr, 0)
        a_pair.start()
        v = columns_end(1)
        rbuf[1, p] = row_sums(v)
        totals_begin(rbuf.at[1], 1)
        totals_begin(rbuf.at[2], 2)
        group_core_end(0, ot)
        t_pair = group_pair(0, ot)
        t_pair.start()
        group_row_end(1, os)
        totals_end(rbuf.at[1], 1)
        u = 1.0 / (all_rows * sum_slots(rbuf.at[1], n_proto))

        columns_begin(2, column_sums(u))
        group_core_begin(1, os)
        a_pair.wait()
        fold_begin(axr, asend, arecv, 0)
        totals_end(rbuf.at[2], 2)
        expo_total = sum_slots(rbuf.at[2], n_proto)
        cot = rc_ref[...] * (1.0 / student_temp)
        over_expo = cot / expo_total
        fbuf[0, y] = over_expo
        rows_begin(fbuf.at[0], f_s.at[0], f_r.at[0])

        def quarter(d):
            return pl.ds(pl.multiple_of(lax.rem(y + d, n_rows) * keep, keep), keep)

        mine = quarter(0)
        t_pair.wait()
        for d in range(others):
            values = jnp.exp(dot(wh[mine, :], ot[d], NN) * (1.0 / teacher_temp))
            shared[d] = values.astype(bf16)
        v = columns_end(2)
        vbuf[...] = v
        part[...] = dot((wht[...].astype(f32) * unfold(v)).astype(bf16), plan[...], NN)
        b_pair = fold_pair(bxs, bxr, 1)
        b_pair.start()
        r3buf[p] = jnp.concatenate(
            [
                row_sums(v),
                fold(jnp.sum(part[...] * sht[...].astype(f32), axis=0, keepdims=True)),
            ],
            axis=0,
        )
        totals_begin(r3buf, 3)
        b_pair.wait()
        fold_begin(bxr, bsend, brecv, 1)

        group_core_end(1, os)
        s_pair = group_pair(1, os)
        s_pair.start()
        s_pair.wait()
        rows_end(fbuf.at[0], f_s.at[0], f_r.at[0])
        for d in range(others):
            values = jnp.exp(dot(wh[mine, :], os[d], NN) * (1.0 / student_temp))
            expo[quarter(d + 1), :] = values.astype(bf16)

        def contract(own, far, e):
            scaled[0] = (sht[...].astype(f32) * unfold(fbuf[e, y])).astype(bf16)
            total = dot(own[mine, :], scaled[0], NT)
            for d in range(1, n_rows):
                factor = unfold(fbuf[e, lax.rem(y + n_rows - d, n_rows)])
                scaled[d] = (os[d - 1].astype(f32) * factor).astype(bf16)
                total = total + dot(far(d), scaled[d], NT)
            return total

        cpart[...] = contract(expo, lambda d: expo[quarter(d), :], 0)
        totals_end(r3buf, 3)
        both = sum_slots(r3buf, n_proto)
        inverse = 1.0 / both[:row_tiles]
        loss_ref[:row_tiles] = jnp.log(expo_total)
        loss_ref[row_tiles:] = both[row_tiles:] * inverse * (1.0 / student_temp)
        over_rows = cot * inverse
        fbuf[1, y] = over_rows
        rows_begin(fbuf.at[1], f_s.at[1], f_r.at[1])

        a_total = fold_end(arecv, 0)
        b_total = fold_end(brecv, 1)

        def half_row(square):
            row = unfold(square)
            return jnp.where(core == 0, row[:, :half], row[:, half:])

        dfull[features, my_half] = (
            a_total * half_row(over_expo) - b_total * half_row(over_rows)
        ).astype(bf16)
        own_piece = dfull.at[features, my_half]
        for offset in core_offsets:
            remote(own_piece, own_piece, s_s.at[2], s_r.at[2], in_plane(offset)).start()

        rows_end(fbuf.at[1], f_s.at[1], f_r.at[1])
        column = column_of(vbuf[pl.ds(pl.multiple_of(y * keep_tiles, keep_tiles), keep_tiles), :])
        total = cpart[...] - column * contract(plan, lambda d: shared[d - 1], 1)
        kept = w_ref[mine, :].astype(f32)
        scale_w = lax.rsqrt(jnp.sum(kept * kept, axis=1, keepdims=True) + epsilon)
        unit_w = kept * scale_w
        gw_ref[...] = (
            (total - unit_w * jnp.sum(unit_w * total, axis=1, keepdims=True)) * scale_w
        ).astype(bf16)

        arrived(dfull.at[all_but_one, my_half], s_s.at[2], s_r.at[2])
        my_pieces = dfull.at[:, my_half]
        d_pair = remote(my_pieces, my_pieces, x_s.at[2], x_r.at[2], sibling)
        d_pair.start()
        d_pair.wait()
        grad_unit = dfull[...].astype(f32)
        unit = srt[...].astype(f32) * scale_s
        gr_ref[...] = (
            (grad_unit - unit * jnp.sum(unit * grad_unit, axis=0, keepdims=True)) * scale_s
        ).astype(bf16)

    scratch = [
        pltpu.VMEM((patches, D), bf16),
        pltpu.VMEM((patches, D), bf16),
        pltpu.VMEM((protos, D), bf16),
        pltpu.VMEM((n_rows, rows, keep), bf16),
        pltpu.VMEM((protos, D), bf16),
        pltpu.VMEM((D, protos), bf16),
        pltpu.VMEM((protos, rows), bf16),
        pltpu.VMEM((protos, rows), bf16),
        pltpu.VMEM((D, rows), bf16),
        pltpu.VMEM((D, rows), bf16),
        pltpu.VMEM((D, rows), bf16),
        pltpu.VMEM((n_rows, D, rows), bf16),
        pltpu.VMEM((D, rows), f32),
        pltpu.VMEM((8, protos), f32),
        pltpu.VMEM((proto_tiles, LANES), f32),
        pltpu.VMEM((3, n_rows, proto_tiles, LANES), f32),
        pltpu.VMEM((3, n_proto, row_tiles, LANES), f32),
        pltpu.VMEM((n_proto, 2 * row_tiles, LANES), f32),
        pltpu.VMEM((2, n_rows, row_tiles, LANES), f32),
        pltpu.VMEM((others, D, rows), bf16),
        pltpu.VMEM((others, D, rows), bf16),
        pltpu.VMEM((keep, D), f32),
        pltpu.VMEM((pairs, chunk, half), bf16),
        pltpu.VMEM((pairs, chunk, half), bf16),
        pltpu.VMEM((D, half), bf16),
        pltpu.VMEM((D, half), bf16),
        pltpu.VMEM((pairs, chunk, half), bf16),
        pltpu.VMEM((pairs, chunk, half), bf16),
        pltpu.VMEM((D, half), bf16),
        pltpu.VMEM((D, half), bf16),
        pltpu.VMEM((D, rows), bf16),
        pltpu.SemaphoreType.DMA((3,)),
        pltpu.SemaphoreType.DMA((3,)),
        pltpu.SemaphoreType.DMA((3,)),
        pltpu.SemaphoreType.DMA((4,)),
        pltpu.SemaphoreType.DMA((4,)),
        pltpu.SemaphoreType.DMA((2,)),
        pltpu.SemaphoreType.DMA((2,)),
        pltpu.SemaphoreType.DMA((2,)),
        pltpu.SemaphoreType.DMA((2,)),
        pltpu.SemaphoreType.DMA((2,)),
        pltpu.SemaphoreType.DMA((2,)),
        pltpu.SemaphoreType.DMA((2,)),
        pltpu.SemaphoreType.DMA((2,)),
        pltpu.SemaphoreType.DMA((3,)),
        pltpu.SemaphoreType.DMA((3,)),
        pltpu.SemaphoreType.DMA((3,)),
        pltpu.SemaphoreType.DMA((3,)),
    ]
    return kernel, scratch


def finish(idx_ref, terms_ref, gr_ref, gw_in, loss_ref, gp_ref, gw_ref):
    step = pl.program_id(0)
    here, rows = gp_ref.shape[0], gr_ref.shape[1]
    spot = lax.broadcasted_iota(jnp.int32, (here, rows), 0) + step * here
    onehot = (spot == unfold(idx_ref[...])).astype(bf16)
    gp_ref[...] = dot(onehot, gr_ref[...], NT)
    gw_ref[...] = gw_in[...].astype(f32)
    tiles = loss_ref.shape[0]
    loss_ref[...] = terms_ref[:tiles] - terms_ref[tiles:]


def shards(student_patches, teacher_patches, mask_index, proto_weight, row_cotangent):
    n_proto, n_rows = lax.axis_size("proto"), lax.axis_size("rows")
    rows = mask_index.shape[0]
    patches = student_patches.shape[0]
    protos = proto_weight.shape[0]
    kernel, scratch = make_kernel(n_proto, n_rows, rows, patches, protos)
    vmem = pl.BlockSpec(memory_space=pltpu.VMEM)
    anywhere = pl.BlockSpec(memory_space=pl.ANY)
    squares = mask_index.reshape(rows // LANES, LANES)
    terms, grad_rows, grad_kept = pl.pallas_call(
        kernel,
        out_shape=(
            jax.ShapeDtypeStruct((2 * rows // LANES, LANES), f32),
            jax.ShapeDtypeStruct((D, rows), bf16),
            jax.ShapeDtypeStruct((protos // n_rows, D), bf16),
        ),
        in_specs=[anywhere, anywhere, vmem, anywhere, vmem],
        out_specs=(vmem, vmem, vmem),
        scratch_shapes=scratch,
        compiler_params=pltpu.CompilerParams(
            collective_id=0, has_side_effects=True, vmem_limit_bytes=60 << 20
        ),
    )(
        student_patches,
        teacher_patches,
        squares,
        proto_weight,
        row_cotangent.reshape(rows // LANES, LANES),
    )
    tiles = rows // LANES
    steps = 4
    loss, grad_patches, grad_weight = pl.pallas_call(
        finish,
        grid=(steps,),
        out_shape=(
            jax.ShapeDtypeStruct((tiles, LANES), f32),
            jax.ShapeDtypeStruct((patches, D), f32),
            jax.ShapeDtypeStruct((protos // n_rows, D), f32),
        ),
        in_specs=[
            pl.BlockSpec((tiles, LANES), lambda i: (0, 0)),
            pl.BlockSpec((2 * tiles, LANES), lambda i: (0, 0)),
            pl.BlockSpec((D, rows), lambda i: (0, 0)),
            pl.BlockSpec((protos // n_rows // steps, D), lambda i: (i, 0)),
        ],
        out_specs=(
            pl.BlockSpec((tiles, LANES), lambda i: (0, 0)),
            pl.BlockSpec((patches // steps, D), lambda i: (i, 0)),
            pl.BlockSpec((protos // n_rows // steps, D), lambda i: (i, 0)),
        ),
        compiler_params=pltpu.CompilerParams(vmem_limit_bytes=60 << 20),
    )(squares, terms, grad_rows, grad_kept)
    return loss.reshape(rows), grad_patches, grad_weight


def solution(mesh):
    in_specs = (P("rows", None), P("rows", None), P("rows"), P("proto", None), P("rows"))
    out_specs = (P("rows"), P("rows", None), P(("proto", "rows"), None))
    return jax.shard_map(shards, mesh=mesh, in_specs=in_specs, out_specs=out_specs, check_vma=False)
```

```python
import itertools
import math

import jax
import jax.numpy as jnp
from jax import lax
from jax.experimental import pallas as pl
from jax.experimental.pallas import tpu as pltpu
from jax.sharding import PartitionSpec as P

teacher_temp = 0.07
student_temp = 0.1
epsilon = 1e-06

f32, bf16 = jnp.float32, jnp.bfloat16
MESH = pl.DeviceIdType.MESH
NN = (((1,), (0,)), ((), ()))
NT = (((1,), (1,)), ((), ()))
TN = (((0,), (0,)), ((), ()))

D = 256
LANES = 128
BLOCK = 256
WIDE = 512


def dot(left, right, dims):
    return lax.dot_general(left, right, dims, preferred_element_type=f32)


def fold(row):
    count = row.shape[1] // LANES
    return jnp.concatenate([row[:, i * LANES : (i + 1) * LANES] for i in range(count)], axis=0)


def unfold(square):
    return jnp.concatenate([square[i : i + 1, :] for i in range(square.shape[0])], axis=1)


def high_low(row):
    high = row.astype(bf16).astype(f32)
    return jnp.concatenate(
        [high, row - high, jnp.zeros((6, row.shape[1]), f32)], axis=0
    ).astype(bf16)


def column_of(square):
    count = square.shape[0]
    padded = jnp.concatenate([square, jnp.zeros((LANES - count, LANES), f32)], axis=0)
    turned = padded.T
    return jnp.concatenate([turned[:, i : i + 1] for i in range(count)], axis=0)


def make_kernel(n_proto, n_rows, rows, patches, protos):
    all_rows = float(rows * n_rows)
    all_protos = float(protos * n_proto)
    keep = protos // n_rows
    row_tiles = rows // LANES
    proto_tiles = protos // LANES
    keep_tiles = keep // LANES
    half = rows // 2
    pairs = n_proto // 2
    chunk = D // pairs
    others = n_rows - 1
    half_tiles = proto_tiles // 2
    side = math.isqrt(pairs)
    assert side * side == pairs and rows == keep

    def hops(offset):
        return sum(min(step, side - step) for step in offset[:2])

    every = itertools.product(range(side), range(side), range(2))
    plane_offsets = sorted((o for o in every if any(o)), key=hops, reverse=True)
    core_offsets = [o for o in plane_offsets if o[2] == 0]
    line_offsets = sorted(range(1, side), key=lambda d: -min(d, side - d))
    share = D // side
    row_offsets = sorted(range(1, n_rows), key=lambda d: -min(d, n_rows - d))

    def kernel(
        sp_any, tp_any, idx_ref, w_any, rc_ref,
        loss_ref, gr_ref, gw_ref,
        sp_ref, tp_ref, w_ref,
        shared, wh, wht, plan, expo, tt, srt, sht, scaled, part, csum, vbuf,
        cbuf, rbuf, fbuf,
        ot, os, cpart,
        asend, arecv, axs, axr, bsend, brecv, bxs, bxr, dfull,
        in_s, y_s, y_r, p_s, p_r, f_s, f_r,
        gy_s, gy_r, gz_s, gz_r, gc_s, gc_r,
        s_s, s_r, x_s, x_r,
    ):
        p = lax.axis_index("proto")
        y = lax.axis_index("rows")
        pair = lax.div(p, 2)
        core = lax.rem(p, 2)
        z = lax.div(pair, side)
        x = lax.rem(pair, side)

        def pair_at(offset):
            return lax.rem(z + offset[0], side) * side + lax.rem(x + offset[1], side)

        def in_plane(offset):
            return (pair_at(offset) * 2 + lax.rem(core + offset[2], 2), y)

        def to_row(d):
            return (p, lax.rem(y + d, n_rows))

        sibling = (p + 1 - 2 * core, y)

        barrier = pltpu.get_barrier_semaphore()
        for offset in plane_offsets:
            pl.semaphore_signal(
                barrier, inc=1, device_id=in_plane(offset), device_id_type=MESH
            )
        for d in range(1, n_rows):
            pl.semaphore_signal(barrier, inc=1, device_id=to_row(d), device_id_type=MESH)

        fetch_t = pltpu.make_async_copy(tp_any, tp_ref, in_s.at[0])
        fetch_w = pltpu.make_async_copy(w_any, w_ref, in_s.at[1])
        fetch_s = pltpu.make_async_copy(sp_any, sp_ref, in_s.at[2])
        fetch_t.start()
        fetch_w.start()
        fetch_s.start()

        def remote(source, target, send, recv, device):
            return pltpu.make_async_remote_copy(
                src_ref=source, dst_ref=target, send_sem=send, recv_sem=recv,
                device_id=device, device_id_type=MESH,
            )

        def arrived(landing, send, recv):
            pltpu.make_async_copy(landing, landing, recv).wait()
            pltpu.make_async_copy(landing, landing, send).wait()

        def totals_begin(buf, e):
            for offset in plane_offsets:
                remote(buf.at[p], buf.at[p], p_s.at[e], p_r.at[e], in_plane(offset)).start()

        def totals_end(buf, e):
            arrived(buf.at[pl.ds(0, n_proto - 1)], p_s.at[e], p_r.at[e])

        def rows_begin(buf, send, recv):
            for d in row_offsets:
                remote(buf.at[y], buf.at[y], send, recv, to_row(d)).start()

        def rows_end(buf, send, recv):
            arrived(buf.at[pl.ds(0, others)], send, recv)

        def sum_slots(buf, count):
            total = buf[0].astype(f32)
            for i in range(1, count):
                total = total + buf[i].astype(f32)
            return total

        features = pl.ds(pl.multiple_of(pair * chunk, chunk), chunk)
        my_half = pl.ds(pl.multiple_of(core * half, half), half)
        other_half = pl.ds(pl.multiple_of((1 - core) * half, half), half)
        all_but_one = pl.ds(0, (pairs - 1) * chunk)

        def carried(e):
            return pl.ds(pl.multiple_of((x, z)[e] * share, share), share)

        def group_row_begin(e, own, far):
            for d in row_offsets:
                remote(
                    own.at[carried(e), my_half], far.at[d - 1, carried(e), my_half],
                    gy_s.at[e], gy_r.at[e], to_row(d),
                ).start()

        def group_row_end(e, far):
            arrived(far.at[:, carried(e), my_half], gy_s.at[e], gy_r.at[e])

        def group_core_begin(e, far):
            piece = far.at[:, carried(e), my_half]
            for step in line_offsets:
                offset = ((0, step, 0), (step, 0, 0))[e]
                remote(piece, piece, gz_s.at[e], gz_r.at[e], in_plane(offset)).start()

        def group_core_end(e, far):
            arrived(far.at[:, pl.ds(0, D - share), my_half], gz_s.at[e], gz_r.at[e])

        def group_pair(e, far):
            piece = far.at[:, :, my_half]
            return remote(piece, piece, gc_s.at[e], gc_r.at[e], sibling)

        idx_row = unfold(idx_ref[...])
        for i in range(patches // rows):
            spot = lax.broadcasted_iota(jnp.int32, (rows, rows), 0) + i * rows
            shared[i] = (spot == idx_row).astype(bf16)

        def masked(patch_ref):
            total = dot(patch_ref[:rows, :], shared[0], TN)
            for i in range(1, patches // rows):
                total = total + dot(patch_ref[i * rows : (i + 1) * rows, :], shared[i], TN)
            return total

        fetch_t.wait()
        teacher = masked(tp_ref)
        tt[...] = (
            teacher * lax.rsqrt(jnp.sum(teacher * teacher, axis=0, keepdims=True) + epsilon)
        ).astype(bf16)

        ones = jnp.ones((8, LANES), bf16)
        fetch_w.wait()

        def plan_block(i, carry):
            at = pl.ds(pl.multiple_of(i * WIDE, WIDE), WIDE)
            block = w_ref[at, :].astype(f32)
            scale = lax.rsqrt(jnp.sum(block * block, axis=1, keepdims=True) + epsilon)
            unit = (block * scale).astype(bf16)
            wh[at, :] = unit
            wht[:, at] = unit.T
            values = jnp.exp(dot(unit, tt[...], NN) * (1.0 / teacher_temp))
            plan[at, :] = values.astype(bf16)
            lane_sum = values[:, :LANES]
            for j in range(1, row_tiles):
                lane_sum = lane_sum + values[:, j * LANES : (j + 1) * LANES]
            high = lane_sum.astype(bf16)
            low = (lane_sum - high.astype(f32)).astype(bf16)
            csum[:, at] = dot(ones, high, NT) + dot(ones, low, NT)
            return carry

        lax.fori_loop(0, protos // WIDE, plan_block, 0, unroll=2)
        pl.semaphore_wait(barrier, n_proto - 1 + n_rows - 1)

        def columns_half(h):
            return pl.ds(h * half_tiles, half_tiles)

        def columns_begin(e, sums_of):
            for h in range(2):
                cbuf[e, y, columns_half(h), :] = fold(sums_of(h))
                mine_here = cbuf.at[e, y, columns_half(h)]
                for d in row_offsets:
                    remote(
                        mine_here, mine_here, y_s.at[e, h], y_r.at[e, h], to_row(d)
                    ).start()

        def columns_end(e, h):
            here = columns_half(h)
            arrived(cbuf.at[e, pl.ds(0, others), here], y_s.at[e, h], y_r.at[e, h])
            total = cbuf[e, 0, here, :]
            for i in range(1, n_rows):
                total = total + cbuf[e, i, here, :]
            return 1.0 / (all_protos * total)

        def plan_half(h):
            return plan[h * (protos // 2) : (h + 1) * (protos // 2), :]

        def both_rows(sums):
            return sums[0:1, :] + sums[1:2, :]

        def row_sums(e):
            sums = jnp.zeros((8, rows), f32)
            for h in range(2):
                v = columns_end(e, h)
                vbuf[h * half_tiles : (h + 1) * half_tiles, :] = v
                sums = sums + dot(high_low(unfold(v)), plan_half(h), NN)
            return fold(both_rows(sums))

        def column_sums(u):
            parts = high_low(unfold(u))
            slots = n_rows // 2

            def sums_of(h):
                sums = [dot(parts, shared[h * slots + i], NN) for i in range(slots)]
                return both_rows(jnp.concatenate(sums, axis=1))

            return sums_of

        def turn(i, carry):
            at = pl.ds(pl.multiple_of(i * BLOCK, BLOCK), BLOCK)
            to = pl.ds(pl.multiple_of(lax.rem(i, keep // BLOCK) * BLOCK, BLOCK), BLOCK)
            shared[lax.div(i, keep // BLOCK), :, to] = plan[at, :].T
            return carry

        turns = protos // BLOCK

        def student_block(i, carry):
            at = pl.ds(pl.multiple_of(i * WIDE, WIDE), WIDE)
            values = jnp.exp(dot(wh[at, :], sht[...], NN) * (1.0 / student_temp))
            expo[at, :] = values.astype(bf16)
            return carry + jnp.sum(values.reshape(WIDE // 8, 8, rows), axis=0)

        columns_begin(0, lambda h: csum[0:1, h * (protos // 2) : (h + 1) * (protos // 2)])
        group_row_begin(0, tt, ot)
        fetch_s.wait()
        student = masked(sp_ref)
        scale_s = lax.rsqrt(jnp.sum(student * student, axis=0, keepdims=True) + epsilon)
        srt[...] = student.astype(bf16)
        sht[...] = (student * scale_s).astype(bf16)
        lax.fori_loop(0, turns // 2, turn, 0, unroll=2)
        rbuf[0, p] = row_sums(0)
        totals_begin(rbuf.at[0], 0)
        group_row_begin(1, sht, os)
        early = protos // WIDE // 2
        expo_rows = lax.fori_loop(
            0, early, student_block, jnp.zeros((8, rows), f32), unroll=2
        )
        lax.fori_loop(turns // 2, turns, turn, 0, unroll=2)
        totals_end(rbuf.at[0], 0)
        u = 1.0 / (all_rows * sum_slots(rbuf.at[0], n_proto))

        columns_begin(1, column_sums(u))
        group_row_end(0, ot)
        group_core_begin(0, ot)
        group_row_end(1, os)
        group_core_begin(1, os)
        expo_rows = lax.fori_loop(early, protos // WIDE, student_block, expo_rows, unroll=2)
        rbuf[2, p] = fold(jnp.sum(expo_rows, axis=0, keepdims=True))

        def fold_pair(xs, xr, e):
            xs[...] = part[:, other_half].astype(bf16)
            return remote(xs, xr, x_s.at[e], x_r.at[e], sibling)

        def fold_begin(xr, send, recv, e):
            total = part[:, my_half] + xr[...].astype(f32)
            send[...] = total.reshape(pairs, chunk, half).astype(bf16)
            for offset in core_offsets:
                remote(
                    send.at[pair_at(offset)], recv.at[pair], s_s.at[e], s_r.at[e],
                    in_plane(offset),
                ).start()
            recv[pair] = send[pair]

        def fold_end(recv, e):
            arrived(recv.at[pl.ds(0, pairs - 1)], s_s.at[e], s_r.at[e])
            return sum_slots(recv, pairs)

        rbuf[1, p] = row_sums(1)
        totals_begin(rbuf.at[1], 1)
        totals_begin(rbuf.at[2], 2)
        part[...] = dot(wht[...], expo[...], NN)
        a_pair = fold_pair(axs, axr, 0)
        a_pair.start()
        group_core_end(0, ot)
        t_pair = group_pair(0, ot)
        t_pair.start()
        group_core_end(1, os)
        s_pair = group_pair(1, os)
        s_pair.start()
        totals_end(rbuf.at[1], 1)
        u = 1.0 / (all_rows * sum_slots(rbuf.at[1], n_proto))

        columns_begin(2, column_sums(u))
        a_pair.wait()
        fold_begin(axr, asend, arecv, 0)
        totals_end(rbuf.at[2], 2)
        expo_total = sum_slots(rbuf.at[2], n_proto)
        cot = rc_ref[...] * (1.0 / student_temp)
        over_expo = cot / expo_total
        fbuf[0, y] = over_expo
        rows_begin(fbuf.at[0], f_s.at[0], f_r.at[0])

        def quarter(d):
            return pl.ds(pl.multiple_of(lax.rem(y + d, n_rows) * keep, keep), keep)

        mine = quarter(0)
        t_pair.wait()
        for d in range(others):
            values = jnp.exp(dot(wh[mine, :], ot[d], NN) * (1.0 / teacher_temp))
            shared[d] = values.astype(bf16)
        rbuf[3, p] = row_sums(2)
        totals_begin(rbuf.at[3], 3)
        for h in range(2):
            v_row = unfold(vbuf[h * half_tiles : (h + 1) * half_tiles, :])
            here = wht[:, h * (protos // 2) : (h + 1) * (protos // 2)].astype(f32)
            piece = dot((here * v_row).astype(bf16), plan_half(h), NN)
            part[...] = piece if h == 0 else part[...] + piece
        b_pair = fold_pair(bxs, bxr, 1)
        b_pair.start()
        rbuf[4, p] = fold(jnp.sum(part[...] * sht[...].astype(f32), axis=0, keepdims=True))
        b_pair.wait()
        fold_begin(bxr, bsend, brecv, 1)
        totals_begin(rbuf.at[4], 4)

        s_pair.wait()
        for d in range(others):
            values = jnp.exp(dot(wh[mine, :], os[d], NN) * (1.0 / student_temp))
            expo[quarter(d + 1), :] = values.astype(bf16)

        def contract_own(own, e):
            scaled[0] = (sht[...].astype(f32) * unfold(fbuf[e, y])).astype(bf16)
            return dot(own[mine, :], scaled[0], NT)

        def contract_far(total, far, e):
            for d in range(1, n_rows):
                factor = unfold(fbuf[e, lax.rem(y + n_rows - d, n_rows)])
                scaled[d] = (os[d - 1].astype(f32) * factor).astype(bf16)
                total = total + dot(far(d), scaled[d], NT)
            return total

        totals_end(rbuf.at[3], 3)
        inverse = 1.0 / sum_slots(rbuf.at[3], n_proto)
        over_rows = cot * inverse
        fbuf[1, y] = over_rows
        rows_begin(fbuf.at[1], f_s.at[1], f_r.at[1])
        rows_end(fbuf.at[0], f_s.at[0], f_r.at[0])
        cpart[...] = contract_far(contract_own(expo, 0), lambda d: expo[quarter(d), :], 0)
        a_total = fold_end(arecv, 0)
        b_total = fold_end(brecv, 1)

        def half_row(square):
            row = unfold(square)
            return jnp.where(core == 0, row[:, :half], row[:, half:])

        dfull[features, my_half] = (
            a_total * half_row(over_expo) - b_total * half_row(over_rows)
        ).astype(bf16)
        own_piece = dfull.at[features, my_half]
        for offset in core_offsets:
            remote(own_piece, own_piece, s_s.at[2], s_r.at[2], in_plane(offset)).start()

        totals_end(rbuf.at[4], 4)
        loss_ref[:row_tiles] = jnp.log(expo_total)
        loss_ref[row_tiles:] = (
            sum_slots(rbuf.at[4], n_proto) * inverse * (1.0 / student_temp)
        )

        own_part = contract_own(plan, 1)
        rows_end(fbuf.at[1], f_s.at[1], f_r.at[1])
        column = column_of(vbuf[pl.ds(pl.multiple_of(y * keep_tiles, keep_tiles), keep_tiles), :])
        total = cpart[...] - column * contract_far(own_part, lambda d: shared[d - 1], 1)
        kept = w_ref[mine, :].astype(f32)
        scale_w = lax.rsqrt(jnp.sum(kept * kept, axis=1, keepdims=True) + epsilon)
        unit_w = kept * scale_w
        gw_ref[...] = (
            (total - unit_w * jnp.sum(unit_w * total, axis=1, keepdims=True)) * scale_w
        ).astype(bf16)

        arrived(dfull.at[all_but_one, my_half], s_s.at[2], s_r.at[2])
        my_pieces = dfull.at[:, my_half]
        d_pair = remote(my_pieces, my_pieces, x_s.at[2], x_r.at[2], sibling)
        d_pair.start()
        d_pair.wait()
        grad_unit = dfull[...].astype(f32)
        unit = srt[...].astype(f32) * scale_s
        gr_ref[...] = (
            (grad_unit - unit * jnp.sum(unit * grad_unit, axis=0, keepdims=True)) * scale_s
        ).astype(bf16).T

    scratch = [
        pltpu.VMEM((patches, D), bf16),
        pltpu.VMEM((patches, D), bf16),
        pltpu.VMEM((protos, D), bf16),
        pltpu.VMEM((n_rows, rows, keep), bf16),
        pltpu.VMEM((protos, D), bf16),
        pltpu.VMEM((D, protos), bf16),
        pltpu.VMEM((protos, rows), bf16),
        pltpu.VMEM((protos, rows), bf16),
        pltpu.VMEM((D, rows), bf16),
        pltpu.VMEM((D, rows), bf16),
        pltpu.VMEM((D, rows), bf16),
        pltpu.VMEM((n_rows, D, rows), bf16),
        pltpu.VMEM((D, rows), f32),
        pltpu.VMEM((8, protos), f32),
        pltpu.VMEM((proto_tiles, LANES), f32),
        pltpu.VMEM((3, n_rows, proto_tiles, LANES), f32),
        pltpu.VMEM((5, n_proto, row_tiles, LANES), f32),
        pltpu.VMEM((2, n_rows, row_tiles, LANES), f32),
        pltpu.VMEM((others, D, rows), bf16),
        pltpu.VMEM((others, D, rows), bf16),
        pltpu.VMEM((keep, D), f32),
        pltpu.VMEM((pairs, chunk, half), bf16),
        pltpu.VMEM((pairs, chunk, half), bf16),
        pltpu.VMEM((D, half), bf16),
        pltpu.VMEM((D, half), bf16),
        pltpu.VMEM((pairs, chunk, half), bf16),
        pltpu.VMEM((pairs, chunk, half), bf16),
        pltpu.VMEM((D, half), bf16),
        pltpu.VMEM((D, half), bf16),
        pltpu.VMEM((D, rows), bf16),
        pltpu.SemaphoreType.DMA((3,)),
        pltpu.SemaphoreType.DMA((3, 2)),
        pltpu.SemaphoreType.DMA((3, 2)),
        pltpu.SemaphoreType.DMA((5,)),
        pltpu.SemaphoreType.DMA((5,)),
        pltpu.SemaphoreType.DMA((2,)),
        pltpu.SemaphoreType.DMA((2,)),
        pltpu.SemaphoreType.DMA((2,)),
        pltpu.SemaphoreType.DMA((2,)),
        pltpu.SemaphoreType.DMA((2,)),
        pltpu.SemaphoreType.DMA((2,)),
        pltpu.SemaphoreType.DMA((2,)),
        pltpu.SemaphoreType.DMA((2,)),
        pltpu.SemaphoreType.DMA((3,)),
        pltpu.SemaphoreType.DMA((3,)),
        pltpu.SemaphoreType.DMA((3,)),
        pltpu.SemaphoreType.DMA((3,)),
    ]
    return kernel, scratch


def finish(idx_ref, terms_ref, gr_ref, gw_in, loss_ref, gp_ref, gw_ref):
    step = pl.program_id(0)
    here, rows = gp_ref.shape[0], gr_ref.shape[0]
    spot = lax.broadcasted_iota(jnp.int32, (here, rows), 0) + step * here
    onehot = (spot == unfold(idx_ref[...])).astype(bf16)
    gp_ref[...] = dot(onehot, gr_ref[...], NN)
    gw_ref[...] = gw_in[...].astype(f32)
    tiles = loss_ref.shape[0]
    loss_ref[...] = terms_ref[:tiles] - terms_ref[tiles:]


def shards(student_patches, teacher_patches, mask_index, proto_weight, row_cotangent):
    n_proto, n_rows = lax.axis_size("proto"), lax.axis_size("rows")
    rows = mask_index.shape[0]
    patches = student_patches.shape[0]
    protos = proto_weight.shape[0]
    kernel, scratch = make_kernel(n_proto, n_rows, rows, patches, protos)
    vmem = pl.BlockSpec(memory_space=pltpu.VMEM)
    anywhere = pl.BlockSpec(memory_space=pl.ANY)
    squares = mask_index.reshape(rows // LANES, LANES)
    terms, grad_rows, grad_kept = pl.pallas_call(
        kernel,
        out_shape=(
            jax.ShapeDtypeStruct((2 * rows // LANES, LANES), f32),
            jax.ShapeDtypeStruct((rows, D), bf16),
            jax.ShapeDtypeStruct((protos // n_rows, D), bf16),
        ),
        in_specs=[anywhere, anywhere, vmem, anywhere, vmem],
        out_specs=(vmem, vmem, vmem),
        scratch_shapes=scratch,
        compiler_params=pltpu.CompilerParams(
            collective_id=0, has_side_effects=True, vmem_limit_bytes=60 << 20
        ),
    )(
        student_patches,
        teacher_patches,
        squares,
        proto_weight,
        row_cotangent.reshape(rows // LANES, LANES),
    )
    tiles = rows // LANES
    steps = 2
    loss, grad_patches, grad_weight = pl.pallas_call(
        finish,
        grid=(steps,),
        out_shape=(
            jax.ShapeDtypeStruct((tiles, LANES), f32),
            jax.ShapeDtypeStruct((patches, D), f32),
            jax.ShapeDtypeStruct((protos // n_rows, D), f32),
        ),
        in_specs=[
            pl.BlockSpec((tiles, LANES), lambda i: (0, 0)),
            pl.BlockSpec((2 * tiles, LANES), lambda i: (0, 0)),
            pl.BlockSpec((rows, D), lambda i: (0, 0)),
            pl.BlockSpec((protos // n_rows // steps, D), lambda i: (i, 0)),
        ],
        out_specs=(
            pl.BlockSpec((tiles, LANES), lambda i: (0, 0)),
            pl.BlockSpec((patches // steps, D), lambda i: (i, 0)),
            pl.BlockSpec((protos // n_rows // steps, D), lambda i: (i, 0)),
        ),
        compiler_params=pltpu.CompilerParams(vmem_limit_bytes=60 << 20),
    )(squares, terms, grad_rows, grad_kept)
    return loss.reshape(rows), grad_patches, grad_weight


def solution(mesh):
    in_specs = (P("rows", None), P("rows", None), P("rows"), P("proto", None), P("rows"))
    out_specs = (P("rows"), P("rows", None), P(("proto", "rows"), None))
    return jax.shard_map(shards, mesh=mesh, in_specs=in_specs, out_specs=out_specs, check_vma=False)
```

```python
import itertools
import math

import jax
import jax.numpy as jnp
from jax import lax
from jax.experimental import pallas as pl
from jax.experimental.pallas import tpu as pltpu
from jax.sharding import PartitionSpec as P

teacher_temp = 0.07
student_temp = 0.1
epsilon = 1e-06

f32, bf16 = jnp.float32, jnp.bfloat16
MESH = pl.DeviceIdType.MESH
NN = (((1,), (0,)), ((), ()))
NT = (((1,), (1,)), ((), ()))
TN = (((0,), (0,)), ((), ()))

D = 256
LANES = 128
BLOCK = 256
WIDE = 512


def dot(left, right, dims):
    return lax.dot_general(left, right, dims, preferred_element_type=f32)


def fold(row):
    count = row.shape[1] // LANES
    return jnp.concatenate([row[:, i * LANES : (i + 1) * LANES] for i in range(count)], axis=0)


def unfold(square):
    return jnp.concatenate([square[i : i + 1, :] for i in range(square.shape[0])], axis=1)


def high_low(row):
    high = row.astype(bf16).astype(f32)
    return jnp.concatenate(
        [high, row - high, jnp.zeros((6, row.shape[1]), f32)], axis=0
    ).astype(bf16)


def column_of(square):
    count = square.shape[0]
    padded = jnp.concatenate([square, jnp.zeros((LANES - count, LANES), f32)], axis=0)
    turned = padded.T
    return jnp.concatenate([turned[:, i : i + 1] for i in range(count)], axis=0)


def make_kernel(n_proto, n_rows, rows, patches, protos):
    all_rows = float(rows * n_rows)
    all_protos = float(protos * n_proto)
    keep = protos // n_rows
    row_tiles = rows // LANES
    proto_tiles = protos // LANES
    keep_tiles = keep // LANES
    half = rows // 2
    pairs = n_proto // 2
    chunk = D // pairs
    others = n_rows - 1
    half_tiles = proto_tiles // 2
    side = math.isqrt(pairs)
    assert side == 4 and side * side == pairs and rows == keep

    def hops(offset):
        return sum(min(step, side - step) for step in offset[:2])

    every = itertools.product(range(side), range(side), range(2))
    plane_offsets = sorted((o for o in every if any(o)), key=hops, reverse=True)
    core_offsets = [o for o in plane_offsets if o[2] == 0]
    share = D // side
    row_offsets = sorted(range(1, n_rows), key=lambda d: -min(d, n_rows - d))

    def kernel(
        sp_any, tp_any, idx_ref, w_any, rc_ref,
        loss_ref, gr_ref, gw_ref,
        sp_ref, tp_ref, w_ref,
        shared, wh, wht, plan, expo, tt, srt, sht, scaled, part, csum, vbuf,
        cbuf, rbuf, fbuf,
        ot, os, cpart,
        asend, arecv, axs, axr, bsend, brecv, bxs, bxr, dfull,
        in_s, y_s, y_r, p_s, p_r, f_s, f_r,
        gy_s, gy_r, gz_s, gz_r, gc_s, gc_r,
        s_s, s_r, x_s, x_r,
    ):
        p = lax.axis_index("proto")
        y = lax.axis_index("rows")
        pair = lax.div(p, 2)
        core = lax.rem(p, 2)
        z = lax.div(pair, side)
        x = lax.rem(pair, side)

        def pair_at(offset):
            return lax.rem(z + offset[0], side) * side + lax.rem(x + offset[1], side)

        def in_plane(offset):
            return (pair_at(offset) * 2 + lax.rem(core + offset[2], 2), y)

        def to_row(d):
            return (p, lax.rem(y + d, n_rows))

        sibling = (p + 1 - 2 * core, y)

        barrier = pltpu.get_barrier_semaphore()
        for offset in plane_offsets:
            pl.semaphore_signal(
                barrier, inc=1, device_id=in_plane(offset), device_id_type=MESH
            )
        for d in range(1, n_rows):
            pl.semaphore_signal(barrier, inc=1, device_id=to_row(d), device_id_type=MESH)

        fetch_t = pltpu.make_async_copy(tp_any, tp_ref, in_s.at[0])
        fetch_w = pltpu.make_async_copy(w_any, w_ref, in_s.at[1])
        fetch_s = pltpu.make_async_copy(sp_any, sp_ref, in_s.at[2])
        fetch_t.start()
        fetch_w.start()
        fetch_s.start()

        def remote(source, target, send, recv, device):
            return pltpu.make_async_remote_copy(
                src_ref=source, dst_ref=target, send_sem=send, recv_sem=recv,
                device_id=device, device_id_type=MESH,
            )

        def arrived(landing, send, recv):
            pltpu.make_async_copy(landing, landing, recv).wait()
            pltpu.make_async_copy(landing, landing, send).wait()

        def totals_begin(buf, e):
            for offset in plane_offsets:
                remote(buf.at[p], buf.at[p], p_s.at[e], p_r.at[e], in_plane(offset)).start()

        def totals_end(buf, e):
            arrived(buf.at[pl.ds(0, n_proto - 1)], p_s.at[e], p_r.at[e])

        def rows_begin(buf, send, recv):
            for d in row_offsets:
                remote(buf.at[y], buf.at[y], send, recv, to_row(d)).start()

        def rows_end(buf, send, recv):
            arrived(buf.at[pl.ds(0, others)], send, recv)

        def sum_slots(buf, count):
            total = buf[0].astype(f32)
            for i in range(1, count):
                total = total + buf[i].astype(f32)
            return total

        features = pl.ds(pl.multiple_of(pair * chunk, chunk), chunk)
        my_half = pl.ds(pl.multiple_of(core * half, half), half)
        other_half = pl.ds(pl.multiple_of((1 - core) * half, half), half)
        all_but_one = pl.ds(0, (pairs - 1) * chunk)

        def carried(e, step=0):
            return pl.ds(pl.multiple_of(lax.rem((x, z)[e] + step, side) * share, share), share)

        def group_row_begin(e, own, far):
            for step in (0, side // 2):
                for d in row_offsets:
                    remote(
                        own.at[carried(e, step), my_half],
                        far.at[d - 1, carried(e, step), my_half],
                        gy_s.at[e], gy_r.at[e], to_row(d),
                    ).start()

        def group_row_end(e, far):
            arrived(far.at[:, pl.ds(0, 2 * share), my_half], gy_s.at[e], gy_r.at[e])

        def group_core_begin(e, far):
            piece = far.at[:, carried(e), my_half]
            for step in (1, side - 1):
                offset = ((0, step, 0), (step, 0, 0))[e]
                remote(piece, piece, gz_s.at[e], gz_r.at[e], in_plane(offset)).start()

        def group_core_end(e, far):
            arrived(far.at[:, pl.ds(0, 2 * share), my_half], gz_s.at[e], gz_r.at[e])

        def group_pair(e, far):
            piece = far.at[:, :, my_half]
            return remote(piece, piece, gc_s.at[e], gc_r.at[e], sibling)

        idx_row = unfold(idx_ref[...])
        for i in range(patches // rows):
            spot = lax.broadcasted_iota(jnp.int32, (rows, rows), 0) + i * rows
            shared[i] = (spot == idx_row).astype(bf16)

        def masked(patch_ref):
            total = dot(patch_ref[:rows, :], shared[0], TN)
            for i in range(1, patches // rows):
                total = total + dot(patch_ref[i * rows : (i + 1) * rows, :], shared[i], TN)
            return total

        fetch_t.wait()
        teacher = masked(tp_ref)
        tt[...] = (
            teacher * lax.rsqrt(jnp.sum(teacher * teacher, axis=0, keepdims=True) + epsilon)
        ).astype(bf16)

        ones = jnp.ones((8, LANES), bf16)
        fetch_w.wait()

        def plan_block(i, carry):
            at = pl.ds(pl.multiple_of(i * WIDE, WIDE), WIDE)
            block = w_ref[at, :].astype(f32)
            scale = lax.rsqrt(jnp.sum(block * block, axis=1, keepdims=True) + epsilon)
            unit = (block * scale).astype(bf16)
            wh[at, :] = unit
            wht[:, at] = unit.T
            values = jnp.exp(dot(unit, tt[...], NN) * (1.0 / teacher_temp))
            plan[at, :] = values.astype(bf16)
            lane_sum = values[:, :LANES]
            for j in range(1, row_tiles):
                lane_sum = lane_sum + values[:, j * LANES : (j + 1) * LANES]
            high = lane_sum.astype(bf16)
            low = (lane_sum - high.astype(f32)).astype(bf16)
            csum[:, at] = dot(ones, high, NT) + dot(ones, low, NT)
            return carry

        lax.fori_loop(0, protos // WIDE, plan_block, 0, unroll=2)
        pl.semaphore_wait(barrier, n_proto - 1 + n_rows - 1)

        def columns_half(h):
            return pl.ds(h * half_tiles, half_tiles)

        def columns_begin(e, sums_of):
            for h in range(2):
                cbuf[e, y, columns_half(h), :] = fold(sums_of(h))
                mine_here = cbuf.at[e, y, columns_half(h)]
                for d in row_offsets:
                    remote(
                        mine_here, mine_here, y_s.at[e, h], y_r.at[e, h], to_row(d)
                    ).start()

        def columns_end(e, h):
            here = columns_half(h)
            arrived(cbuf.at[e, pl.ds(0, others), here], y_s.at[e, h], y_r.at[e, h])
            total = cbuf[e, 0, here, :]
            for i in range(1, n_rows):
                total = total + cbuf[e, i, here, :]
            return 1.0 / (all_protos * total)

        def plan_half(h):
            return plan[h * (protos // 2) : (h + 1) * (protos // 2), :]

        def both_rows(sums):
            return sums[0:1, :] + sums[1:2, :]

        def row_sums(e):
            sums = jnp.zeros((8, rows), f32)
            for h in range(2):
                v = columns_end(e, h)
                vbuf[h * half_tiles : (h + 1) * half_tiles, :] = v
                sums = sums + dot(high_low(unfold(v)), plan_half(h), NN)
            return fold(both_rows(sums))

        def column_sums(u):
            parts = high_low(unfold(u))
            slots = n_rows // 2

            def sums_of(h):
                sums = [dot(parts, shared[h * slots + i], NN) for i in range(slots)]
                return both_rows(jnp.concatenate(sums, axis=1))

            return sums_of

        def turn(i, carry):
            at = pl.ds(pl.multiple_of(i * BLOCK, BLOCK), BLOCK)
            to = pl.ds(pl.multiple_of(lax.rem(i, keep // BLOCK) * BLOCK, BLOCK), BLOCK)
            shared[lax.div(i, keep // BLOCK), :, to] = plan[at, :].T
            return carry

        turns = protos // BLOCK

        def student_block(i, carry):
            at = pl.ds(pl.multiple_of(i * WIDE, WIDE), WIDE)
            values = jnp.exp(dot(wh[at, :], sht[...], NN) * (1.0 / student_temp))
            expo[at, :] = values.astype(bf16)
            return carry + jnp.sum(values.reshape(WIDE // 8, 8, rows), axis=0)

        columns_begin(0, lambda h: csum[0:1, h * (protos // 2) : (h + 1) * (protos // 2)])
        group_row_begin(0, tt, ot)
        fetch_s.wait()
        student = masked(sp_ref)
        scale_s = lax.rsqrt(jnp.sum(student * student, axis=0, keepdims=True) + epsilon)
        srt[...] = student.astype(bf16)
        sht[...] = (student * scale_s).astype(bf16)
        lax.fori_loop(0, turns // 2, turn, 0, unroll=2)
        rbuf[0, p] = row_sums(0)
        totals_begin(rbuf.at[0], 0)
        group_row_begin(1, sht, os)
        early = protos // WIDE // 2
        expo_rows = lax.fori_loop(
            0, early, student_block, jnp.zeros((8, rows), f32), unroll=2
        )
        lax.fori_loop(turns // 2, turns, turn, 0, unroll=2)
        totals_end(rbuf.at[0], 0)
        u = 1.0 / (all_rows * sum_slots(rbuf.at[0], n_proto))

        group_row_end(0, ot)
        group_core_begin(0, ot)
        columns_begin(1, column_sums(u))
        group_row_end(1, os)
        group_core_begin(1, os)
        expo_rows = lax.fori_loop(early, protos // WIDE, student_block, expo_rows, unroll=2)
        rbuf[2, p] = fold(jnp.sum(expo_rows, axis=0, keepdims=True))

        def fold_pair(xs, xr, e):
            xs[...] = part[:, other_half].astype(bf16)
            return remote(xs, xr, x_s.at[e], x_r.at[e], sibling)

        def fold_begin(xr, send, recv, e):
            total = part[:, my_half] + xr[...].astype(f32)
            send[...] = total.reshape(pairs, chunk, half).astype(bf16)
            for offset in core_offsets:
                remote(
                    send.at[pair_at(offset)], recv.at[pair], s_s.at[e], s_r.at[e],
                    in_plane(offset),
                ).start()
            recv[pair] = send[pair]

        def fold_end(recv, e):
            arrived(recv.at[pl.ds(0, pairs - 1)], s_s.at[e], s_r.at[e])
            return sum_slots(recv, pairs)

        rbuf[1, p] = row_sums(1)
        totals_begin(rbuf.at[1], 1)
        totals_begin(rbuf.at[2], 2)
        part[...] = dot(wht[...], expo[...], NN)
        a_pair = fold_pair(axs, axr, 0)
        a_pair.start()
        group_core_end(0, ot)
        t_pair = group_pair(0, ot)
        t_pair.start()
        group_core_end(1, os)
        s_pair = group_pair(1, os)
        s_pair.start()
        totals_end(rbuf.at[1], 1)
        u = 1.0 / (all_rows * sum_slots(rbuf.at[1], n_proto))

        columns_begin(2, column_sums(u))
        a_pair.wait()
        fold_begin(axr, asend, arecv, 0)
        totals_end(rbuf.at[2], 2)
        expo_total = sum_slots(rbuf.at[2], n_proto)
        cot = rc_ref[...] * (1.0 / student_temp)
        over_expo = cot / expo_total
        fbuf[0, y] = over_expo
        rows_begin(fbuf.at[0], f_s.at[0], f_r.at[0])

        def quarter(d):
            return pl.ds(pl.multiple_of(lax.rem(y + d, n_rows) * keep, keep), keep)

        mine = quarter(0)
        t_pair.wait()
        for d in range(others):
            values = jnp.exp(dot(wh[mine, :], ot[d], NN) * (1.0 / teacher_temp))
            shared[d] = values.astype(bf16)
        rbuf[3, p] = row_sums(2)
        totals_begin(rbuf.at[3], 3)
        for h in range(2):
            v_row = unfold(vbuf[h * half_tiles : (h + 1) * half_tiles, :])
            here = wht[:, h * (protos // 2) : (h + 1) * (protos // 2)].astype(f32)
            piece = dot((here * v_row).astype(bf16), plan_half(h), NN)
            part[...] = piece if h == 0 else part[...] + piece
        b_pair = fold_pair(bxs, bxr, 1)
        b_pair.start()
        rbuf[4, p] = fold(jnp.sum(part[...] * sht[...].astype(f32), axis=0, keepdims=True))
        b_pair.wait()
        fold_begin(bxr, bsend, brecv, 1)
        totals_begin(rbuf.at[4], 4)

        s_pair.wait()
        for d in range(others):
            values = jnp.exp(dot(wh[mine, :], os[d], NN) * (1.0 / student_temp))
            expo[quarter(d + 1), :] = values.astype(bf16)

        def contract_own(own, e):
            scaled[0] = (sht[...].astype(f32) * unfold(fbuf[e, y])).astype(bf16)
            return dot(own[mine, :], scaled[0], NT)

        def contract_far(total, far, e):
            for d in range(1, n_rows):
                factor = unfold(fbuf[e, lax.rem(y + n_rows - d, n_rows)])
                scaled[d] = (os[d - 1].astype(f32) * factor).astype(bf16)
                total = total + dot(far(d), scaled[d], NT)
            return total

        totals_end(rbuf.at[3], 3)
        inverse = 1.0 / sum_slots(rbuf.at[3], n_proto)
        over_rows = cot * inverse
        fbuf[1, y] = over_rows
        rows_begin(fbuf.at[1], f_s.at[1], f_r.at[1])
        rows_end(fbuf.at[0], f_s.at[0], f_r.at[0])
        cpart[...] = contract_far(contract_own(expo, 0), lambda d: expo[quarter(d), :], 0)
        a_total = fold_end(arecv, 0)
        b_total = fold_end(brecv, 1)

        def half_row(square):
            row = unfold(square)
            return jnp.where(core == 0, row[:, :half], row[:, half:])

        dfull[features, my_half] = (
            a_total * half_row(over_expo) - b_total * half_row(over_rows)
        ).astype(bf16)
        own_piece = dfull.at[features, my_half]
        for offset in core_offsets:
            remote(own_piece, own_piece, s_s.at[2], s_r.at[2], in_plane(offset)).start()

        totals_end(rbuf.at[4], 4)
        loss_ref[:row_tiles] = jnp.log(expo_total)
        loss_ref[row_tiles:] = (
            sum_slots(rbuf.at[4], n_proto) * inverse * (1.0 / student_temp)
        )

        own_part = contract_own(plan, 1)
        rows_end(fbuf.at[1], f_s.at[1], f_r.at[1])
        column = column_of(vbuf[pl.ds(pl.multiple_of(y * keep_tiles, keep_tiles), keep_tiles), :])
        total = cpart[...] - column * contract_far(own_part, lambda d: shared[d - 1], 1)
        kept = w_ref[mine, :].astype(f32)
        scale_w = lax.rsqrt(jnp.sum(kept * kept, axis=1, keepdims=True) + epsilon)
        unit_w = kept * scale_w
        gw_ref[...] = (
            (total - unit_w * jnp.sum(unit_w * total, axis=1, keepdims=True)) * scale_w
        ).astype(bf16)

        arrived(dfull.at[all_but_one, my_half], s_s.at[2], s_r.at[2])
        my_pieces = dfull.at[:, my_half]
        d_pair = remote(my_pieces, my_pieces, x_s.at[2], x_r.at[2], sibling)
        d_pair.start()
        d_pair.wait()
        grad_unit = dfull[...].astype(f32)
        unit = srt[...].astype(f32) * scale_s
        gr_ref[...] = (
            (grad_unit - unit * jnp.sum(unit * grad_unit, axis=0, keepdims=True)) * scale_s
        ).astype(bf16).T

    scratch = [
        pltpu.VMEM((patches, D), bf16),
        pltpu.VMEM((patches, D), bf16),
        pltpu.VMEM((protos, D), bf16),
        pltpu.VMEM((n_rows, rows, keep), bf16),
        pltpu.VMEM((protos, D), bf16),
        pltpu.VMEM((D, protos), bf16),
        pltpu.VMEM((protos, rows), bf16),
        pltpu.VMEM((protos, rows), bf16),
        pltpu.VMEM((D, rows), bf16),
        pltpu.VMEM((D, rows), bf16),
        pltpu.VMEM((D, rows), bf16),
        pltpu.VMEM((n_rows, D, rows), bf16),
        pltpu.VMEM((D, rows), f32),
        pltpu.VMEM((8, protos), f32),
        pltpu.VMEM((proto_tiles, LANES), f32),
        pltpu.VMEM((3, n_rows, proto_tiles, LANES), f32),
        pltpu.VMEM((5, n_proto, row_tiles, LANES), f32),
        pltpu.VMEM((2, n_rows, row_tiles, LANES), f32),
        pltpu.VMEM((others, D, rows), bf16),
        pltpu.VMEM((others, D, rows), bf16),
        pltpu.VMEM((keep, D), f32),
        pltpu.VMEM((pairs, chunk, half), bf16),
        pltpu.VMEM((pairs, chunk, half), bf16),
        pltpu.VMEM((D, half), bf16),
        pltpu.VMEM((D, half), bf16),
        pltpu.VMEM((pairs, chunk, half), bf16),
        pltpu.VMEM((pairs, chunk, half), bf16),
        pltpu.VMEM((D, half), bf16),
        pltpu.VMEM((D, half), bf16),
        pltpu.VMEM((D, rows), bf16),
        pltpu.SemaphoreType.DMA((3,)),
        pltpu.SemaphoreType.DMA((3, 2)),
        pltpu.SemaphoreType.DMA((3, 2)),
        pltpu.SemaphoreType.DMA((5,)),
        pltpu.SemaphoreType.DMA((5,)),
        pltpu.SemaphoreType.DMA((2,)),
        pltpu.SemaphoreType.DMA((2,)),
        pltpu.SemaphoreType.DMA((2,)),
        pltpu.SemaphoreType.DMA((2,)),
        pltpu.SemaphoreType.DMA((2,)),
        pltpu.SemaphoreType.DMA((2,)),
        pltpu.SemaphoreType.DMA((2,)),
        pltpu.SemaphoreType.DMA((2,)),
        pltpu.SemaphoreType.DMA((3,)),
        pltpu.SemaphoreType.DMA((3,)),
        pltpu.SemaphoreType.DMA((3,)),
        pltpu.SemaphoreType.DMA((3,)),
    ]
    return kernel, scratch


def finish(idx_ref, terms_ref, gr_ref, gw_in, loss_ref, gp_ref, gw_ref):
    step = pl.program_id(0)
    here, rows = gp_ref.shape[0], gr_ref.shape[0]
    spot = lax.broadcasted_iota(jnp.int32, (here, rows), 0) + step * here
    onehot = (spot == unfold(idx_ref[...])).astype(bf16)
    gp_ref[...] = dot(onehot, gr_ref[...], NN)
    gw_ref[...] = gw_in[...].astype(f32)
    tiles = loss_ref.shape[0]
    loss_ref[...] = terms_ref[:tiles] - terms_ref[tiles:]


def shards(student_patches, teacher_patches, mask_index, proto_weight, row_cotangent):
    n_proto, n_rows = lax.axis_size("proto"), lax.axis_size("rows")
    rows = mask_index.shape[0]
    patches = student_patches.shape[0]
    protos = proto_weight.shape[0]
    kernel, scratch = make_kernel(n_proto, n_rows, rows, patches, protos)
    vmem = pl.BlockSpec(memory_space=pltpu.VMEM)
    anywhere = pl.BlockSpec(memory_space=pl.ANY)
    squares = mask_index.reshape(rows // LANES, LANES)
    terms, grad_rows, grad_kept = pl.pallas_call(
        kernel,
        out_shape=(
            jax.ShapeDtypeStruct((2 * rows // LANES, LANES), f32),
            jax.ShapeDtypeStruct((rows, D), bf16),
            jax.ShapeDtypeStruct((protos // n_rows, D), bf16),
        ),
        in_specs=[anywhere, anywhere, vmem, anywhere, vmem],
        out_specs=(vmem, vmem, vmem),
        scratch_shapes=scratch,
        compiler_params=pltpu.CompilerParams(
            collective_id=0, has_side_effects=True, vmem_limit_bytes=60 << 20
        ),
    )(
        student_patches,
        teacher_patches,
        squares,
        proto_weight,
        row_cotangent.reshape(rows // LANES, LANES),
    )
    tiles = rows // LANES
    steps = 2
    loss, grad_patches, grad_weight = pl.pallas_call(
        finish,
        grid=(steps,),
        out_shape=(
            jax.ShapeDtypeStruct((tiles, LANES), f32),
            jax.ShapeDtypeStruct((patches, D), f32),
            jax.ShapeDtypeStruct((protos // n_rows, D), f32),
        ),
        in_specs=[
            pl.BlockSpec((tiles, LANES), lambda i: (0, 0)),
            pl.BlockSpec((2 * tiles, LANES), lambda i: (0, 0)),
            pl.BlockSpec((rows, D), lambda i: (0, 0)),
            pl.BlockSpec((protos // n_rows // steps, D), lambda i: (i, 0)),
        ],
        out_specs=(
            pl.BlockSpec((tiles, LANES), lambda i: (0, 0)),
            pl.BlockSpec((patches // steps, D), lambda i: (i, 0)),
            pl.BlockSpec((protos // n_rows // steps, D), lambda i: (i, 0)),
        ),
        compiler_params=pltpu.CompilerParams(vmem_limit_bytes=60 << 20),
    )(squares, terms, grad_rows, grad_kept)
    return loss.reshape(rows), grad_patches, grad_weight


def solution(mesh):
    in_specs = (P("rows", None), P("rows", None), P("rows"), P("proto", None), P("rows"))
    out_specs = (P("rows"), P("rows", None), P(("proto", "rows"), None))
    return jax.shard_map(shards, mesh=mesh, in_specs=in_specs, out_specs=out_specs, check_vma=False)
```

```python
import itertools
import math

import jax
import jax.numpy as jnp
from jax import lax
from jax.experimental import pallas as pl
from jax.experimental.pallas import tpu as pltpu
from jax.sharding import PartitionSpec as P

teacher_temp = 0.07
student_temp = 0.1
epsilon = 1e-06

f32, bf16 = jnp.float32, jnp.bfloat16
MESH = pl.DeviceIdType.MESH
NN = (((1,), (0,)), ((), ()))
NT = (((1,), (1,)), ((), ()))
TN = (((0,), (0,)), ((), ()))

D = 256
LANES = 128
BLOCK = 256
WIDE = 512


def dot(left, right, dims):
    return lax.dot_general(left, right, dims, preferred_element_type=f32)


def fold(row):
    count = row.shape[1] // LANES
    return jnp.concatenate([row[:, i * LANES : (i + 1) * LANES] for i in range(count)], axis=0)


def unfold(square):
    return jnp.concatenate([square[i : i + 1, :] for i in range(square.shape[0])], axis=1)


def high_low(row):
    high = row.astype(bf16).astype(f32)
    return jnp.concatenate(
        [high, row - high, jnp.zeros((6, row.shape[1]), f32)], axis=0
    ).astype(bf16)


def column_of(square):
    count = square.shape[0]
    padded = jnp.concatenate([square, jnp.zeros((LANES - count, LANES), f32)], axis=0)
    turned = padded.T
    return jnp.concatenate([turned[:, i : i + 1] for i in range(count)], axis=0)


def make_kernel(n_proto, n_rows, rows, patches, protos):
    all_rows = float(rows * n_rows)
    all_protos = float(protos * n_proto)
    keep = protos // n_rows
    row_tiles = rows // LANES
    proto_tiles = protos // LANES
    keep_tiles = keep // LANES
    half = rows // 2
    pairs = n_proto // 2
    chunk = D // pairs
    others = n_rows - 1
    half_tiles = proto_tiles // 2
    side = math.isqrt(pairs)
    assert side == 4 and side * side == pairs and rows == keep

    def hops(offset):
        return sum(min(step, side - step) for step in offset[:2])

    every = itertools.product(range(side), range(side), range(2))
    plane_offsets = sorted((o for o in every if any(o)), key=hops, reverse=True)
    core_offsets = [o for o in plane_offsets if o[2] == 0]
    share = D // side
    row_offsets = sorted(range(1, n_rows), key=lambda d: -min(d, n_rows - d))

    def kernel(
        sp_any, tp_any, idx_ref, w_any, rc_ref,
        loss_ref, gr_ref, gw_ref,
        sp_ref, tp_ref, w_ref,
        shared, wh, wht, plan, expo, tt, srt, sht, scaled, part, csum, vbuf,
        cbuf, rbuf, fbuf,
        ot, os, cpart,
        asend, arecv, axs, axr, bsend, brecv, bxs, bxr, dfull,
        in_s, y_s, y_r, p_s, p_r, f_s, f_r,
        gy_s, gy_r, gz_s, gz_r, gc_s, gc_r,
        s_s, s_r, x_s, x_r,
    ):
        p = lax.axis_index("proto")
        y = lax.axis_index("rows")
        pair = lax.div(p, 2)
        core = lax.rem(p, 2)
        z = lax.div(pair, side)
        x = lax.rem(pair, side)

        def pair_at(offset):
            return lax.rem(z + offset[0], side) * side + lax.rem(x + offset[1], side)

        def in_plane(offset):
            return (pair_at(offset) * 2 + lax.rem(core + offset[2], 2), y)

        def to_row(d):
            return (p, lax.rem(y + d, n_rows))

        sibling = (p + 1 - 2 * core, y)

        barrier = pltpu.get_barrier_semaphore()
        for offset in plane_offsets:
            pl.semaphore_signal(
                barrier, inc=1, device_id=in_plane(offset), device_id_type=MESH
            )
        for d in range(1, n_rows):
            pl.semaphore_signal(barrier, inc=1, device_id=to_row(d), device_id_type=MESH)

        fetch_t = pltpu.make_async_copy(tp_any, tp_ref, in_s.at[0])
        fetch_w = pltpu.make_async_copy(w_any, w_ref, in_s.at[1])
        fetch_s = pltpu.make_async_copy(sp_any, sp_ref, in_s.at[2])
        fetch_t.start()
        fetch_w.start()
        fetch_s.start()

        def remote(source, target, send, recv, device):
            return pltpu.make_async_remote_copy(
                src_ref=source, dst_ref=target, send_sem=send, recv_sem=recv,
                device_id=device, device_id_type=MESH,
            )

        def arrived(landing, send, recv):
            pltpu.make_async_copy(landing, landing, recv).wait()
            pltpu.make_async_copy(landing, landing, send).wait()

        def totals_begin(buf, e):
            for offset in plane_offsets:
                remote(buf.at[p], buf.at[p], p_s.at[e], p_r.at[e], in_plane(offset)).start()

        def totals_end(buf, e):
            arrived(buf.at[pl.ds(0, n_proto - 1)], p_s.at[e], p_r.at[e])

        def rows_begin(buf, send, recv):
            for d in row_offsets:
                remote(buf.at[y], buf.at[y], send, recv, to_row(d)).start()

        def rows_end(buf, send, recv):
            arrived(buf.at[pl.ds(0, others)], send, recv)

        def sum_slots(buf, count):
            total = buf[0].astype(f32)
            for i in range(1, count):
                total = total + buf[i].astype(f32)
            return total

        features = pl.ds(pl.multiple_of(pair * chunk, chunk), chunk)
        my_half = pl.ds(pl.multiple_of(core * half, half), half)
        other_half = pl.ds(pl.multiple_of((1 - core) * half, half), half)
        all_but_one = pl.ds(0, (pairs - 1) * chunk)

        def carried(e, step=0):
            return pl.ds(pl.multiple_of(lax.rem((x, z)[e] + step, side) * share, share), share)

        def group_row_begin(e, own, far):
            for step in (0, side // 2):
                for d in row_offsets:
                    remote(
                        own.at[carried(e, step), my_half],
                        far.at[d - 1, carried(e, step), my_half],
                        gy_s.at[e], gy_r.at[e], to_row(d),
                    ).start()

        def group_row_end(e, far):
            arrived(far.at[:, pl.ds(0, 2 * share), my_half], gy_s.at[e], gy_r.at[e])

        def group_core_begin(e, far):
            piece = far.at[:, carried(e), my_half]
            for step in (1, side - 1):
                offset = ((0, step, 0), (step, 0, 0))[e]
                remote(piece, piece, gz_s.at[e], gz_r.at[e], in_plane(offset)).start()

        def group_core_end(e, far):
            arrived(far.at[:, pl.ds(0, 2 * share), my_half], gz_s.at[e], gz_r.at[e])

        def group_pair(e, far):
            piece = far.at[:, :, my_half]
            return remote(piece, piece, gc_s.at[e], gc_r.at[e], sibling)

        idx_row = unfold(idx_ref[...])
        for i in range(patches // rows):
            spot = lax.broadcasted_iota(jnp.int32, (rows, rows), 0) + i * rows
            shared[i] = (spot == idx_row).astype(bf16)

        def masked(patch_ref):
            total = dot(patch_ref[:rows, :], shared[0], TN)
            for i in range(1, patches // rows):
                total = total + dot(patch_ref[i * rows : (i + 1) * rows, :], shared[i], TN)
            return total

        fetch_t.wait()
        teacher = masked(tp_ref)
        tt[...] = (
            teacher * lax.rsqrt(jnp.sum(teacher * teacher, axis=0, keepdims=True) + epsilon)
        ).astype(bf16)

        ones = jnp.ones((8, LANES), bf16)
        fetch_w.wait()

        def plan_block(i, carry):
            at = pl.ds(pl.multiple_of(i * WIDE, WIDE), WIDE)
            block = w_ref[at, :].astype(f32)
            scale = lax.rsqrt(jnp.sum(block * block, axis=1, keepdims=True) + epsilon)
            unit = (block * scale).astype(bf16)
            wh[at, :] = unit
            wht[:, at] = unit.T
            values = jnp.exp(dot(unit, tt[...], NN) * (1.0 / teacher_temp))
            plan[at, :] = values.astype(bf16)
            lane_sum = values[:, :LANES]
            for j in range(1, row_tiles):
                lane_sum = lane_sum + values[:, j * LANES : (j + 1) * LANES]
            high = lane_sum.astype(bf16)
            low = (lane_sum - high.astype(f32)).astype(bf16)
            csum[:, at] = dot(ones, high, NT) + dot(ones, low, NT)
            return carry

        lax.fori_loop(0, protos // WIDE, plan_block, 0, unroll=2)
        pl.semaphore_wait(barrier, n_proto - 1 + n_rows - 1)

        def columns_half(h):
            return pl.ds(h * half_tiles, half_tiles)

        def columns_begin(e, sums_of):
            for h in range(2):
                cbuf[e, y, columns_half(h), :] = fold(sums_of(h))
                mine_here = cbuf.at[e, y, columns_half(h)]
                for d in row_offsets:
                    remote(
                        mine_here, mine_here, y_s.at[e, h], y_r.at[e, h], to_row(d)
                    ).start()

        def columns_end(e, h):
            here = columns_half(h)
            arrived(cbuf.at[e, pl.ds(0, others), here], y_s.at[e, h], y_r.at[e, h])
            total = cbuf[e, 0, here, :]
            for i in range(1, n_rows):
                total = total + cbuf[e, i, here, :]
            return 1.0 / (all_protos * total)

        def plan_half(h):
            return plan[h * (protos // 2) : (h + 1) * (protos // 2), :]

        def both_rows(sums):
            return sums[0:1, :] + sums[1:2, :]

        def row_sums(e):
            sums = jnp.zeros((8, rows), f32)
            for h in range(2):
                v = columns_end(e, h)
                vbuf[h * half_tiles : (h + 1) * half_tiles, :] = v
                sums = sums + dot(high_low(unfold(v)), plan_half(h), NN)
            return fold(both_rows(sums))

        def column_sums(u):
            parts = high_low(unfold(u))
            slots = n_rows // 2

            def sums_of(h):
                sums = [dot(parts, shared[h * slots + i], NN) for i in range(slots)]
                return both_rows(jnp.concatenate(sums, axis=1))

            return sums_of

        def turn(i, carry):
            at = pl.ds(pl.multiple_of(i * BLOCK, BLOCK), BLOCK)
            to = pl.ds(pl.multiple_of(lax.rem(i, keep // BLOCK) * BLOCK, BLOCK), BLOCK)
            shared[lax.div(i, keep // BLOCK), :, to] = plan[at, :].T
            return carry

        turns = protos // BLOCK

        def student_block(i, carry):
            at = pl.ds(pl.multiple_of(i * WIDE, WIDE), WIDE)
            values = jnp.exp(dot(wh[at, :], sht[...], NN) * (1.0 / student_temp))
            expo[at, :] = values.astype(bf16)
            return carry + jnp.sum(values.reshape(WIDE // 8, 8, rows), axis=0)

        columns_begin(0, lambda h: csum[0:1, h * (protos // 2) : (h + 1) * (protos // 2)])
        group_row_begin(0, tt, ot)
        fetch_s.wait()
        student = masked(sp_ref)
        scale_s = lax.rsqrt(jnp.sum(student * student, axis=0, keepdims=True) + epsilon)
        srt[...] = student.astype(bf16)
        sht[...] = (student * scale_s).astype(bf16)
        lax.fori_loop(0, turns // 2, turn, 0, unroll=2)
        rbuf[0, p] = row_sums(0)
        totals_begin(rbuf.at[0], 0)
        group_row_begin(1, sht, os)
        early = protos // WIDE // 2
        expo_rows = lax.fori_loop(
            0, early, student_block, jnp.zeros((8, rows), f32), unroll=2
        )
        lax.fori_loop(turns // 2, turns, turn, 0, unroll=2)
        totals_end(rbuf.at[0], 0)
        u = 1.0 / (all_rows * sum_slots(rbuf.at[0], n_proto))

        group_row_end(0, ot)
        group_core_begin(0, ot)
        columns_begin(1, column_sums(u))
        group_row_end(1, os)
        group_core_begin(1, os)
        expo_rows = lax.fori_loop(early, protos // WIDE, student_block, expo_rows, unroll=2)
        rbuf[2, p] = fold(jnp.sum(expo_rows, axis=0, keepdims=True))

        def fold_pair(xs, xr, e):
            xs[...] = part[:, other_half].astype(bf16)
            return remote(xs, xr, x_s.at[e], x_r.at[e], sibling)

        def fold_begin(xr, send, recv, e):
            total = part[:, my_half] + xr[...].astype(f32)
            send[...] = total.reshape(pairs, chunk, half).astype(bf16)
            for offset in core_offsets:
                remote(
                    send.at[pair_at(offset)], recv.at[pair], s_s.at[e], s_r.at[e],
                    in_plane(offset),
                ).start()
            recv[pair] = send[pair]

        def fold_end(recv, e):
            arrived(recv.at[pl.ds(0, pairs - 1)], s_s.at[e], s_r.at[e])
            return sum_slots(recv, pairs)

        rbuf[1, p] = row_sums(1)
        totals_begin(rbuf.at[1], 1)
        totals_begin(rbuf.at[2], 2)
        part[...] = dot(wht[...], expo[...], NN)
        a_pair = fold_pair(axs, axr, 0)
        a_pair.start()
        group_core_end(0, ot)
        t_pair = group_pair(0, ot)
        t_pair.start()
        group_core_end(1, os)
        s_pair = group_pair(1, os)
        s_pair.start()
        totals_end(rbuf.at[1], 1)
        u = 1.0 / (all_rows * sum_slots(rbuf.at[1], n_proto))

        columns_begin(2, column_sums(u))
        a_pair.wait()
        fold_begin(axr, asend, arecv, 0)
        totals_end(rbuf.at[2], 2)
        expo_total = sum_slots(rbuf.at[2], n_proto)
        cot = rc_ref[...] * (1.0 / student_temp)
        over_expo = cot / expo_total
        fbuf[0, y] = over_expo
        rows_begin(fbuf.at[0], f_s.at[0], f_r.at[0])

        def quarter(d):
            return pl.ds(pl.multiple_of(lax.rem(y + d, n_rows) * keep, keep), keep)

        mine = quarter(0)
        t_pair.wait()
        for d in range(others):
            values = jnp.exp(dot(wh[mine, :], ot[d], NN) * (1.0 / teacher_temp))
            shared[d] = values.astype(bf16)
        rbuf[3, p] = row_sums(2)
        totals_begin(rbuf.at[3], 3)
        for h in range(2):
            v_row = unfold(vbuf[h * half_tiles : (h + 1) * half_tiles, :])
            here = wht[:, h * (protos // 2) : (h + 1) * (protos // 2)].astype(f32)
            piece = dot((here * v_row).astype(bf16), plan_half(h), NN)
            part[...] = piece if h == 0 else part[...] + piece
        b_pair = fold_pair(bxs, bxr, 1)
        b_pair.start()
        rbuf[4, p] = fold(jnp.sum(part[...] * sht[...].astype(f32), axis=0, keepdims=True))
        b_pair.wait()
        fold_begin(bxr, bsend, brecv, 1)
        totals_begin(rbuf.at[4], 4)

        s_pair.wait()
        for d in range(others):
            values = jnp.exp(dot(wh[mine, :], os[d], NN) * (1.0 / student_temp))
            expo[quarter(d + 1), :] = values.astype(bf16)

        def contract_own(own, e):
            scaled[0] = (sht[...].astype(f32) * unfold(fbuf[e, y])).astype(bf16)
            return dot(own[mine, :], scaled[0], NT)

        def contract_far(total, far, e):
            for d in range(1, n_rows):
                factor = unfold(fbuf[e, lax.rem(y + n_rows - d, n_rows)])
                scaled[d] = (os[d - 1].astype(f32) * factor).astype(bf16)
                total = total + dot(far(d), scaled[d], NT)
            return total

        totals_end(rbuf.at[3], 3)
        inverse = 1.0 / sum_slots(rbuf.at[3], n_proto)
        over_rows = cot * inverse
        fbuf[1, y] = over_rows
        rows_begin(fbuf.at[1], f_s.at[1], f_r.at[1])
        rows_end(fbuf.at[0], f_s.at[0], f_r.at[0])
        cpart[...] = contract_far(contract_own(expo, 0), lambda d: expo[quarter(d), :], 0)
        a_total = fold_end(arecv, 0)
        b_total = fold_end(brecv, 1)

        def half_row(square):
            row = unfold(square)
            return jnp.where(core == 0, row[:, :half], row[:, half:])

        dfull[features, my_half] = (
            a_total * half_row(over_expo) - b_total * half_row(over_rows)
        ).astype(bf16)
        own_piece = dfull.at[features, my_half]
        for offset in core_offsets:
            remote(own_piece, own_piece, s_s.at[2], s_r.at[2], in_plane(offset)).start()

        totals_end(rbuf.at[4], 4)
        loss_ref[:row_tiles] = jnp.log(expo_total)
        loss_ref[row_tiles:] = (
            sum_slots(rbuf.at[4], n_proto) * inverse * (1.0 / student_temp)
        )

        own_part = contract_own(plan, 1)
        rows_end(fbuf.at[1], f_s.at[1], f_r.at[1])
        column = column_of(vbuf[pl.ds(pl.multiple_of(y * keep_tiles, keep_tiles), keep_tiles), :])
        total = cpart[...] - column * contract_far(own_part, lambda d: shared[d - 1], 1)
        arrived(dfull.at[all_but_one, my_half], s_s.at[2], s_r.at[2])
        my_pieces = dfull.at[:, my_half]
        d_pair = remote(my_pieces, my_pieces, x_s.at[2], x_r.at[2], sibling)
        d_pair.start()
        kept = w_ref[mine, :].astype(f32)
        scale_w = lax.rsqrt(jnp.sum(kept * kept, axis=1, keepdims=True) + epsilon)
        unit_w = kept * scale_w
        gw_ref[...] = (
            (total - unit_w * jnp.sum(unit_w * total, axis=1, keepdims=True)) * scale_w
        ).astype(bf16)

        d_pair.wait()
        grad_unit = dfull[...].astype(f32)
        unit = srt[...].astype(f32) * scale_s
        gr_ref[...] = (
            (grad_unit - unit * jnp.sum(unit * grad_unit, axis=0, keepdims=True)) * scale_s
        ).astype(bf16).T

    scratch = [
        pltpu.VMEM((patches, D), bf16),
        pltpu.VMEM((patches, D), bf16),
        pltpu.VMEM((protos, D), bf16),
        pltpu.VMEM((n_rows, rows, keep), bf16),
        pltpu.VMEM((protos, D), bf16),
        pltpu.VMEM((D, protos), bf16),
        pltpu.VMEM((protos, rows), bf16),
        pltpu.VMEM((protos, rows), bf16),
        pltpu.VMEM((D, rows), bf16),
        pltpu.VMEM((D, rows), bf16),
        pltpu.VMEM((D, rows), bf16),
        pltpu.VMEM((n_rows, D, rows), bf16),
        pltpu.VMEM((D, rows), f32),
        pltpu.VMEM((8, protos), f32),
        pltpu.VMEM((proto_tiles, LANES), f32),
        pltpu.VMEM((3, n_rows, proto_tiles, LANES), f32),
        pltpu.VMEM((5, n_proto, row_tiles, LANES), f32),
        pltpu.VMEM((2, n_rows, row_tiles, LANES), f32),
        pltpu.VMEM((others, D, rows), bf16),
        pltpu.VMEM((others, D, rows), bf16),
        pltpu.VMEM((keep, D), f32),
        pltpu.VMEM((pairs, chunk, half), bf16),
        pltpu.VMEM((pairs, chunk, half), bf16),
        pltpu.VMEM((D, half), bf16),
        pltpu.VMEM((D, half), bf16),
        pltpu.VMEM((pairs, chunk, half), bf16),
        pltpu.VMEM((pairs, chunk, half), bf16),
        pltpu.VMEM((D, half), bf16),
        pltpu.VMEM((D, half), bf16),
        pltpu.VMEM((D, rows), bf16),
        pltpu.SemaphoreType.DMA((3,)),
        pltpu.SemaphoreType.DMA((3, 2)),
        pltpu.SemaphoreType.DMA((3, 2)),
        pltpu.SemaphoreType.DMA((5,)),
        pltpu.SemaphoreType.DMA((5,)),
        pltpu.SemaphoreType.DMA((2,)),
        pltpu.SemaphoreType.DMA((2,)),
        pltpu.SemaphoreType.DMA((2,)),
        pltpu.SemaphoreType.DMA((2,)),
        pltpu.SemaphoreType.DMA((2,)),
        pltpu.SemaphoreType.DMA((2,)),
        pltpu.SemaphoreType.DMA((2,)),
        pltpu.SemaphoreType.DMA((2,)),
        pltpu.SemaphoreType.DMA((3,)),
        pltpu.SemaphoreType.DMA((3,)),
        pltpu.SemaphoreType.DMA((3,)),
        pltpu.SemaphoreType.DMA((3,)),
    ]
    return kernel, scratch


def finish(idx_ref, terms_ref, gr_ref, gw_in, loss_ref, gp_ref, gw_ref):
    step = pl.program_id(0)
    here, rows = gp_ref.shape[0], gr_ref.shape[0]
    spot = lax.broadcasted_iota(jnp.int32, (here, rows), 0) + step * here
    onehot = (spot == unfold(idx_ref[...])).astype(bf16)
    gp_ref[...] = dot(onehot, gr_ref[...], NN)
    gw_ref[...] = gw_in[...].astype(f32)
    tiles = loss_ref.shape[0]
    loss_ref[...] = terms_ref[:tiles] - terms_ref[tiles:]


def shards(student_patches, teacher_patches, mask_index, proto_weight, row_cotangent):
    n_proto, n_rows = lax.axis_size("proto"), lax.axis_size("rows")
    rows = mask_index.shape[0]
    patches = student_patches.shape[0]
    protos = proto_weight.shape[0]
    kernel, scratch = make_kernel(n_proto, n_rows, rows, patches, protos)
    vmem = pl.BlockSpec(memory_space=pltpu.VMEM)
    anywhere = pl.BlockSpec(memory_space=pl.ANY)
    squares = mask_index.reshape(rows // LANES, LANES)
    terms, grad_rows, grad_kept = pl.pallas_call(
        kernel,
        out_shape=(
            jax.ShapeDtypeStruct((2 * rows // LANES, LANES), f32),
            jax.ShapeDtypeStruct((rows, D), bf16),
            jax.ShapeDtypeStruct((protos // n_rows, D), bf16),
        ),
        in_specs=[anywhere, anywhere, vmem, anywhere, vmem],
        out_specs=(vmem, vmem, vmem),
        scratch_shapes=scratch,
        compiler_params=pltpu.CompilerParams(
            collective_id=0, has_side_effects=True, vmem_limit_bytes=60 << 20
        ),
    )(
        student_patches,
        teacher_patches,
        squares,
        proto_weight,
        row_cotangent.reshape(rows // LANES, LANES),
    )
    tiles = rows // LANES
    steps = 2
    loss, grad_patches, grad_weight = pl.pallas_call(
        finish,
        grid=(steps,),
        out_shape=(
            jax.ShapeDtypeStruct((tiles, LANES), f32),
            jax.ShapeDtypeStruct((patches, D), f32),
            jax.ShapeDtypeStruct((protos // n_rows, D), f32),
        ),
        in_specs=[
            pl.BlockSpec((tiles, LANES), lambda i: (0, 0)),
            pl.BlockSpec((2 * tiles, LANES), lambda i: (0, 0)),
            pl.BlockSpec((rows, D), lambda i: (0, 0)),
            pl.BlockSpec((protos // n_rows // steps, D), lambda i: (i, 0)),
        ],
        out_specs=(
            pl.BlockSpec((tiles, LANES), lambda i: (0, 0)),
            pl.BlockSpec((patches // steps, D), lambda i: (i, 0)),
            pl.BlockSpec((protos // n_rows // steps, D), lambda i: (i, 0)),
        ),
        compiler_params=pltpu.CompilerParams(vmem_limit_bytes=60 << 20),
    )(squares, terms, grad_rows, grad_kept)
    return loss.reshape(rows), grad_patches, grad_weight


def solution(mesh):
    in_specs = (P("rows", None), P("rows", None), P("rows"), P("proto", None), P("rows"))
    out_specs = (P("rows"), P("rows", None), P(("proto", "rows"), None))
    return jax.shard_map(shards, mesh=mesh, in_specs=in_specs, out_specs=out_specs, check_vma=False)
```
